32 devices in a mesh: gx: 8 (over y, x, core), gy: 4 (over z).
Axes of the slice: x: 2, y: 2, z: 4, core: 2. Of those that a mesh axis runs over, the one named last changes fastest.
Arguments:
- checkpoint: float32 [19, 64, 256, 128], P(None, 'gx', 'gy'), may hold values from 0 to 1, as said below
- fluid: int32 [64, 256, 128], P('gx', 'gy'), may hold values 0 or 1
- adjoint_in: float32 [19, 64, 256, 128], P(None, 'gx', 'gy'), may hold values from -6 to 6
Outputs:
- state: float32 [19, 64, 256, 128], P(None, 'gx', 'gy')
- adjoint: float32 [19, 64, 256, 128], P(None, 'gx', 'gy')
The draws below stay inside these ranges and needn't reach their ends.
Inputs may be any that keep to these rules, and one draw needn't show every extreme that they name: `checkpoint`: positive populations near equilibrium. 1 marks a fluid cell, 0 a solid one.
All inputs are finite; a program needn't handle non-finite values. No bound on the sum of `fluid` on one device may be relied on, other than what follows from the above.
Results may differ from the reference program's by a relative error of at most 0.0003.
Values sent between devices are 32-bit elements; how exact they have to be, the bound alone decides.
A program may use at most 128 MiB of HBM per device.

```python
import jax
import jax.numpy as jnp
import numpy as np
from jax import lax

Q = 19
NZ = 128
STEPS = 3
NX = 64
NY = 256


VELOCITY = [(0, 0, 0), (1, 0, 0), (-1, 0, 0), (0, 1, 0), (0, -1, 0), (0, 0, 1), (0, 0, -1), (1, 1, 0), (-1, -1, 0), (1, -1, 0), (-1, 1, 0), (1, 0, 1), (-1, 0, -1), (1, 0, -1), (-1, 0, 1), (0, 1, 1), (0, -1, -1), (0, 1, -1), (0, -1, 1)]


WEIGHTS = [1.0 / 3.0] + [1.0 / 18.0] * 6 + [1.0 / 36.0] * 12


def draw_checkpoint(key, part):
    key_density = jax.random.fold_in(key, 11)
    key_flow = jax.random.fold_in(key, 12)
    key_noise = jax.random.fold_in(key, 13)
    density = jax.random.uniform(key_density, (NX, NY, NZ), jnp.float32, 0.9, 1.1)
    flow = jax.random.uniform(key_flow, (3, NX, NY, NZ), jnp.float32, -0.08, 0.08)
    noise = jax.random.uniform(key_noise, (19, NX, NY, NZ), jnp.float32, -0.15, 0.15)
    speeds = jnp.array(VELOCITY, jnp.float32)
    along = speeds[:, 0, None, None, None] * flow[0][None] + speeds[:, 1, None, None, None] * flow[1][None] + speeds[:, 2, None, None, None] * flow[2][None]
    weights = jnp.array(WEIGHTS, jnp.float32)[:, None, None, None]
    return (weights * density[None] * (1.0 + 3.0 * along + noise)).astype(jnp.float32)


def with_ends(result, key, least, largest):
    place = [jax.random.randint(jax.random.fold_in(key, axis), (), 0, length) for axis, length in enumerate(result.shape)]
    longest = result.shape.index(max(result.shape))
    neighbour = place[:longest] + [(place[longest] + 1) % result.shape[longest]] + place[longest + 1:]
    return result.at[tuple(place)].set(least).at[tuple(neighbour)].set(largest)


def block_levels(own_key, extent, split, least, largest):
    def one(axis_at, shards_of):
        heights = jax.random.uniform(jax.random.fold_in(jax.random.fold_in(own_key, 6), axis_at), (shards_of,), jnp.float32, least / len(split), largest / len(split))
        return jnp.repeat(jnp.exp(heights), extent[axis_at] // shards_of).reshape((-1,) + (1,) * (len(extent) - axis_at - 1))

    factor_of = one(*split[0])
    for cut in split[1:]:
        factor_of = factor_of * one(*cut)
    return factor_of


def normal_values(key, extent, spread, bound, split=(), dtype=jnp.bfloat16):
    values = jax.random.normal(key, extent, jnp.float32) * spread
    if len(split) > 0:
        values = block_levels(key, extent, split, -0.22, 0.18) * values
    return jnp.clip(values, min=-bound, max=bound).astype(dtype)


def setup_inputs(seed: int = 0) -> dict:
    key_of = jax.random.split(jax.random.key(seed), 4)
    return {
        "checkpoint": draw_checkpoint(jax.random.fold_in(key_of[3], 71), 0),
        "fluid": with_ends((jax.random.randint(key_of[1], (NX, NY, NZ), 0, 10) < 9).astype(jnp.int32), jax.random.fold_in(key_of[1], 1), 0, 1),
        "adjoint_in": normal_values(key_of[2], (Q, NX, NY, NZ), 1.0, 6.0, ((1, 8), (2, 4)), jnp.float32),
    }


VELOCITY = [(0, 0, 0), (1, 0, 0), (-1, 0, 0), (0, 1, 0), (0, -1, 0), (0, 0, 1), (0, 0, -1), (1, 1, 0), (-1, -1, 0), (1, -1, 0), (-1, 1, 0), (1, 0, 1), (-1, 0, -1), (1, 0, -1), (-1, 0, 1), (0, 1, 1), (0, -1, -1), (0, 1, -1), (0, -1, 1)]
WEIGHTS = [1.0 / 3.0] + [1.0 / 18.0] * 6 + [1.0 / 36.0] * 12
OPPOSITE = [0, 2, 1, 4, 3, 6, 5, 8, 7, 10, 9, 12, 11, 14, 13, 16, 15, 18, 17]
RELAXATION = 1.6

def collide(values):
    speeds = jnp.array(VELOCITY, jnp.float32)
    weights = jnp.array(WEIGHTS, jnp.float32)[:, None, None, None]
    density = lax.optimization_barrier(jnp.sum(values, axis=0))
    moment = jnp.einsum('qc,qxyz->cxyz', speeds, values, precision=lax.Precision.HIGHEST)
    flow = moment / density
    along = jnp.einsum('qc,cxyz->qxyz', speeds, flow, precision=lax.Precision.HIGHEST)
    square = lax.optimization_barrier(jnp.sum(flow * flow, axis=0))
    balance = weights * density * (1.0 + 3.0 * along + 4.5 * along * along - 1.5 * square)
    return values - RELAXATION * (values - balance)

def source(plane, speed):
    moved = jnp.roll(plane, (speed[0], speed[1]), (0, 1))
    if speed[2] == 1:
        moved = jnp.concatenate([jnp.zeros_like(moved[:, :, :1]), moved[:, :, :-1]], 2)
    elif speed[2] == -1:
        moved = jnp.concatenate([moved[:, :, 1:], jnp.zeros_like(moved[:, :, :1])], 2)
    return moved

def advance(values, fluid):
    posted = collide(values)
    fluid_float = fluid.astype(jnp.float32)
    read = jnp.stack([source(posted[channel], VELOCITY[channel]) for channel in range(19)])
    open_source = jnp.stack([source(fluid_float, VELOCITY[channel]) for channel in range(19)]) > 0.5
    bounced = posted[np.array(OPPOSITE)]
    inside = jnp.where(open_source, read, bounced)
    return jnp.where(fluid_float[None] > 0.5, inside, values)

def reference(checkpoint, fluid, adjoint_in):
    current = checkpoint
    for step_index in range(STEPS):
        current = advance(current, fluid)
    _, pull_back = jax.vjp(lambda values: advance(values, fluid), current)
    adjoint, = pull_back(adjoint_in)
    return (current, adjoint)
```

```python
import jax
import jax.numpy as jnp
from jax import lax
from jax.experimental import pallas as pl
from jax.experimental.pallas import tpu as pltpu
from jax.sharding import PartitionSpec as P

VELOCITY = [
    (0, 0, 0),
    (1, 0, 0),
    (-1, 0, 0),
    (0, 1, 0),
    (0, -1, 0),
    (0, 0, 1),
    (0, 0, -1),
    (1, 1, 0),
    (-1, -1, 0),
    (1, -1, 0),
    (-1, 1, 0),
    (1, 0, 1),
    (-1, 0, -1),
    (1, 0, -1),
    (-1, 0, 1),
    (0, 1, 1),
    (0, -1, -1),
    (0, 1, -1),
    (0, -1, 1),
]
OPPOSITE = [0, 2, 1, 4, 3, 6, 5, 8, 7, 10, 9, 12, 11, 14, 13, 16, 15, 18, 17]
ORDER = [0, 1, 7, 9, 11, 13, 2, 8, 10, 12, 14, 3, 4, 5, 6, 15, 16, 17, 18]
SLOT = [ORDER.index(q) for q in range(19)]
UP = [3, 7, 10, 15, 17]
DOWN = [4, 8, 9, 16, 18]
CORNER = [7, 8, 9, 10]
PAD = 8
T = 8
MIB = 1 << 20


def shifted(ref, q, x, y, speed):
    row = PAD + T * y - speed[1]
    tile = ref[SLOT[q], x + 1 - speed[0], row : row + T, :]
    if speed[2]:
        tile = pltpu.roll(tile, speed[2] % tile.shape[1], 1)
    return tile


def own(ref, q, x, y):
    return ref[SLOT[q], x + 1, PAD + T * y : PAD + T * y + T, :]


def stream(ref, bits, x, y):
    result = [own(ref, 0, x, y)]
    for q in range(1, 19):
        is_open = (bits & (1 << q)) != 0
        result.append(
            jnp.where(is_open, shifted(ref, q, x, y, VELOCITY[q]), own(ref, OPPOSITE[q], x, y))
        )
    return result


def moments(v):
    s = {q: v[q] + v[q + 1] for q in range(1, 19, 2)}
    d = {q: v[q] - v[q + 1] for q in range(1, 19, 2)}
    rho = v[0] + ((s[1] + s[3]) + (s[5] + s[7])) + ((s[9] + s[11]) + (s[13] + (s[15] + s[17])))
    mx = d[1] + (d[7] + d[9]) + (d[11] + d[13])
    my = d[3] + (d[7] - d[9]) + (d[15] + d[17])
    mz = d[5] + (d[11] - d[13]) + (d[15] - d[17])
    return rho, mx, my, mz


def collide(v):
    rho, mx, my, mz = moments(v)
    inverse = 3.0 / rho
    ux, uy, uz = mx * inverse, my * inverse, mz * inverse
    base = 1.0 - (ux * ux + uy * uy + uz * uz) * (1.0 / 6.0)
    along = {
        1: ux,
        3: uy,
        5: uz,
        7: ux + uy,
        9: ux - uy,
        11: ux + uz,
        13: ux - uz,
        15: uy + uz,
        17: uy - uz,
    }
    axis, diagonal = rho * (1.6 / 18.0), rho * (1.6 / 36.0)
    result = [rho * (1.6 / 3.0) * base - 0.6 * v[0]]
    for q in range(1, 19, 2):
        a = along[q]
        even = base + 0.5 * (a * a)
        factor = axis if q < 7 else diagonal
        result.append(factor * (even + a) - 0.6 * v[q])
        result.append(factor * (even - a) - 0.6 * v[q + 1])
    return result


def pull_back(v, b):
    rho, mx, my, mz = moments(v)
    inverse = 1.0 / rho
    ux, uy, uz = mx * inverse, my * inverse, mz * inverse
    s = {q: b[q] + b[q + 1] for q in range(1, 19, 2)}
    d = {q: b[q] - b[q + 1] for q in range(1, 19, 2)}
    for q in (1, 3, 5):
        s[q] = s[q] + s[q]
        d[q] = d[q] + d[q]
    sxy_p, sxz_p, syz_p = s[7] + s[9], s[11] + s[13], s[15] + s[17]
    sxy, sxz, syz = s[7] - s[9], s[11] - s[13], s[15] - s[17]
    s0 = 12.0 * b[0] + (s[1] + s[3]) + (s[5] + sxy_p) + (sxz_p + syz_p)
    sxx, syy, szz = s[1] + sxy_p + sxz_p, s[3] + sxy_p + syz_p, s[5] + sxz_p + syz_p
    s1x = d[1] + (d[7] + d[9]) + (d[11] + d[13])
    s1y = d[3] + (d[7] - d[9]) + (d[15] + d[17])
    s1z = d[5] + (d[11] - d[13]) + (d[15] - d[17])
    tx = sxx * ux + sxy * uy + sxz * uz
    ty = sxy * ux + syy * uy + syz * uz
    tz = sxz * ux + syz * uy + szz * uz
    k = 1.6 / 36.0
    square = ux * ux + uy * uy + uz * uz
    level = k * (s0 * (1.0 + 1.5 * square) - 4.5 * (ux * tx + uy * ty + uz * tz))
    gx = (3.0 * k) * (s1x + 3.0 * tx - ux * s0)
    gy = (3.0 * k) * (s1y + 3.0 * ty - uy * s0)
    gz = (3.0 * k) * (s1z + 3.0 * tz - uz * s0)
    along = {
        1: gx,
        3: gy,
        5: gz,
        7: gx + gy,
        9: gx - gy,
        11: gx + gz,
        13: gx - gz,
        15: gy + gz,
        17: gy - gz,
    }
    result = [level - 0.6 * b[0]]
    for q in range(1, 19, 2):
        result.append((level + along[q]) - 0.6 * b[q])
        result.append((level - along[q]) - 0.6 * b[q + 1])
    return result


SLOW, FAST = 0, 1
LOW, HIGH, MIDDLE, OTHER, Y_SLOW, Y_REST, DIAGONAL = 0, 1, 2, 3, 4, 6, 8
LANES = 12


def forward_kernel(
    start_ref, fluid_ref, seed_ref,
    state_ref, adjoint_ref,
    post_1, post_2, post_3, held, bits_ref, start, cells, solid,
    y_send, y_recv, c_send, c_recv,
    load_sem, send_sem, recv_sem, seed_send, seed_recv,
):
    _, nx, ny, nz = start_ref.shape
    tiles = ny // T
    last = tiles - 1
    top = PAD + ny
    me = {"gx": lax.axis_index("gx"), "gy": lax.axis_index("gy")}
    count = {"gx": lax.axis_size("gx"), "gy": lax.axis_size("gy")}
    odd = lax.rem(me["gx"], 2)
    sign = {SLOW: odd, FAST: 1 - odd}
    face = {side: (nx - 1) * p for side, p in sign.items()}
    rest = pl.ds(1 - odd, nx - 1)

    def first_of(p):
        return 6 - 5 * p

    def corner_of(p, up):
        return 8 - 6 * p if up else 7 - 4 * p

    def halo_of(p):
        return (nx + 1) * (1 - p)

    def device(dx, dy):
        to_x = lax.rem(me["gx"] + dx + count["gx"], count["gx"])
        to_y = lax.rem(me["gy"] + dy + count["gy"], count["gy"])
        return (to_x, to_y)

    def toward(side, dy):
        return device(2 * sign[side] - 1, dy)

    around = [(i, j) for i in (-1, 0, 1) for j in (-1, 0, 1) if (i, j) != (0, 0)]
    barrier = pltpu.get_barrier_semaphore()
    for i, j in around:
        pl.semaphore_signal(barrier, inc=1, device_id=device(i, j), device_id_type=pl.DeviceIdType.MESH)

    fluid_load = pltpu.make_async_copy(fluid_ref, cells, load_sem.at[0])
    fluid_load.start()
    start_load = [
        pltpu.make_async_copy(start_ref.at[:, planes], start.at[:, planes], load_sem.at[1 + i])
        for i, planes in enumerate((pl.ds(face[SLOW], 1), pl.ds(face[FAST], 1), pl.ds(1, nx - 2)))
    ]
    for load in start_load:
        load.start()
    seed_load = [
        pltpu.make_async_copy(
            seed_ref.at[q],
            held.at[SLOT[OPPOSITE[q]], pl.ds(1, nx), pl.ds(PAD, ny)],
            load_sem.at[4 + q],
        )
        for q in range(19)
    ]

    def remote(source, target, send, receive, to):
        return pltpu.make_async_remote_copy(
            src_ref=source, dst_ref=target, send_sem=send, recv_sem=receive,
            device_id=to, device_id_type=pl.DeviceIdType.MESH,
        )

    seed_faces = {
        side: [
            remote(
                seed_ref.at[2 * k + 5 + p if k else 1 + p, face[side]],
                held.at[first_of(p) + k, halo_of(p), pl.ds(PAD, ny)],
                seed_send.at[side, k], seed_recv.at[side, k], toward(side, 0),
            )
            for k in range(5)
        ]
        for side, p in sign.items()
    }

    def face_copy(e, lane, ref, side, first_tile, end_tile):
        p = sign[side]
        five, rows = pl.ds(first_of(p), 5), pl.ds(PAD + T * first_tile, T * (end_tile - first_tile))
        return remote(
            ref.at[five, face[side] + 1, rows], ref.at[five, halo_of(p), rows],
            send_sem.at[e, lane], recv_sem.at[e, lane], toward(side, 0),
        )

    def row_copies(e, lane, planes):
        return [
            remote(
                y_send.at[e, i, planes], y_recv.at[e, i, planes],
                send_sem.at[e, lane + i], recv_sem.at[e, lane + i], device(0, 1 - 2 * i),
            )
            for i in range(2)
        ]

    def corner_copies(e, side):
        return [
            remote(
                c_send.at[e, 2 * side + i], c_recv.at[e, 2 * side + i],
                send_sem.at[e, DIAGONAL + 2 * side + i], recv_sem.at[e, DIAGONAL + 2 * side + i],
                toward(side, 1 - 2 * i),
            )
            for i in range(2)
        ]

    def pack_plane(e, ref, x):
        for k in range(5):
            y_send[e, 0, x, k] = ref[SLOT[UP[k]], x + 1, top - 1 : top, :]
            y_send[e, 1, x, k] = ref[SLOT[DOWN[k]], x + 1, PAD : PAD + 1, :]

    def unpack_plane(e, ref, x):
        for k in range(5):
            ref[SLOT[UP[k]], x + 1, PAD - 1 : PAD, :] = y_recv[e, 0, x, k]
            ref[SLOT[DOWN[k]], x + 1, top : top + 1, :] = y_recv[e, 1, x, k]

    def sweep(begin_at, length, body):
        def one(i, _):
            body(begin_at + i)
            return 0

        lax.fori_loop(0, length, one, 0)

    def pack_corners(e, ref, side):
        p = sign[side]
        c_send[e, 2 * side] = ref[corner_of(p, True), face[side] + 1, top - 1 : top, :]
        c_send[e, 2 * side + 1] = ref[corner_of(p, False), face[side] + 1, PAD : PAD + 1, :]

    def unpack_corners(e, ref, side):
        p = 1 - sign[side]
        ref[corner_of(p, True), halo_of(p), PAD - 1 : PAD, :] = c_recv[e, 2 * side]
        ref[corner_of(p, False), halo_of(p), top : top + 1, :] = c_recv[e, 2 * side + 1]

    sent = []

    def begin(made):
        for copy in made:
            copy.start()
        sent.extend(made)

    def arrive(made):
        for copy in made:
            copy.wait_recv()

    fluid_load.wait()

    def to_float(x):
        solid[x + 1, PAD:top, :] = cells[x].astype(jnp.float32)
        y_send[0, 0, x, 0] = solid[x + 1, top - 1 : top, :]
        y_send[0, 1, x, 0] = solid[x + 1, PAD : PAD + 1, :]

    sweep(0, nx, to_float)
    for side in (SLOW, FAST):
        c_send[0, 2 * side] = solid[face[side] + 1, top - 1 : top, :]
        c_send[0, 2 * side + 1] = solid[face[side] + 1, PAD : PAD + 1, :]
    pl.semaphore_wait(barrier, len(around))
    cell_copies = [
        remote(
            solid.at[face[side] + 1, pl.ds(PAD, ny)], solid.at[halo_of(sign[side]), pl.ds(PAD, ny)],
            send_sem.at[0, side], recv_sem.at[0, side], toward(side, 0),
        )
        for side in (SLOW, FAST)
    ]
    for i in range(2):
        cell_copies.append(
            remote(
                y_send.at[0, i, :, 0], y_recv.at[0, i, :, 0],
                send_sem.at[0, Y_SLOW + i], recv_sem.at[0, Y_SLOW + i], device(0, 1 - 2 * i),
            )
        )
    cell_copies += corner_copies(0, SLOW) + corner_copies(0, FAST)
    begin(cell_copies)

    def store(to, x, y, v, is_fluid):
        for q, value in enumerate(collide(v)):
            to[SLOT[q], x + 1, PAD + T * y : PAD + T * y + T, :] = jnp.where(
                is_fluid, value, v[OPPOSITE[q]]
            )

    def first(x, y):
        v = [start[q, x, T * y : T * y + T, :] for q in range(19)]
        store(post_1, x, y, v, solid[x + 1, PAD + T * y : PAD + T * y + T, :] > 0.5)

    def middle(source, to):
        def body(x, y):
            bits = bits_ref[x, T * y : T * y + T, :]
            v = stream(source, bits, x, y)
            store(to, x, y, v, (bits & 1) != 0)

        return body

    def edge_line(body):
        def line(x):
            body(x, 0)
            body(x, last)

        return line

    def inner_line(body):
        def line(x):
            for y in range(1, last):
                body(x, y)

        return line

    def sweep_edges(body):
        sweep(1, nx - 2, edge_line(body))

    def sweep_interior(body):
        sweep(1, nx - 2, inner_line(body))

    def slow_copies(e, ref):
        outer = 4 - e
        return {
            "outer": [
                face_copy(e, LOW, ref, SLOW, 0, outer),
                face_copy(e, HIGH, ref, SLOW, tiles - outer, tiles),
            ],
            "middle": [face_copy(e, MIDDLE, ref, SLOW, outer, tiles - outer)],
            "corners": corner_copies(e, SLOW),
            "rows": row_copies(e, Y_SLOW, pl.ds(face[SLOW], 1)),
        }

    def send_outer(e, to, body):
        made = slow_copies(e, to)
        outer = 4 - e
        for i in range(outer):
            body(face[SLOW], i)
            body(face[SLOW], last - i)
            if i == 0:
                pack_corners(e, to, SLOW)
                pack_plane(e, to, face[SLOW])
                begin(made["corners"] + made["rows"])
        begin(made["outer"])
        return made

    def send_middle(e, made, body):
        outer = 4 - e
        for y in range(outer, tiles - outer):
            body(face[SLOW], y)
        begin(made["middle"])

    def other_copies(e, ref):
        return {
            "face": [face_copy(e, OTHER, ref, FAST, 0, tiles)] + corner_copies(e, FAST),
            "rows": row_copies(e, Y_REST, rest),
        }

    def send_fast(e, to, body):
        made = other_copies(e, to)
        for y in range(tiles):
            body(face[FAST], y)
        pack_corners(e, to, FAST)
        begin(made["face"])
        return made

    def send_rows(e, to, made):
        sweep(1 - odd, nx - 1, lambda x: pack_plane(e, to, x))
        begin(made["rows"])

    def take_rows(e, ref, slow, other):
        arrive(slow["rows"] + other["rows"])
        sweep(0, nx, lambda x: unpack_plane(e, ref, x))

    def take_fast(e, ref, made):
        arrive(made["face"])
        unpack_corners(e, ref, FAST)

    def take_outer(e, ref, made):
        arrive(made["corners"])
        unpack_corners(e, ref, SLOW)
        arrive(made["outer"])

    start_load[0].wait()
    slow_1 = send_outer(1, post_1, first)
    send_middle(1, slow_1, first)
    begin(seed_faces[SLOW][:2])
    start_load[1].wait()
    fast_1 = send_fast(1, post_1, first)
    start_load[2].wait()
    for load in seed_load:
        load.start()
    sweep_edges(first)
    send_rows(1, post_1, fast_1)
    sweep_interior(first)

    layer = lax.broadcasted_iota(jnp.int32, (T, nz), 1)
    inside = {1: (layer > 0).astype(jnp.float32), -1: (layer < nz - 1).astype(jnp.float32)}

    def mark(x, y):
        flat, up, down = 1.0, 0.0, 0.0
        for q in range(1, 19):
            c = VELOCITY[q]
            row = PAD + T * y - c[1]
            tile = solid[x + 1 - c[0], row : row + T, :] * float(1 << q)
            if c[2] == 0:
                flat = flat + tile
            elif c[2] == 1:
                up = up + tile
            else:
                down = down + tile
        total = flat + pltpu.roll(up, 1, 1) * inside[1] + pltpu.roll(down, nz - 1, 1) * inside[-1]
        here = solid[x + 1, PAD + T * y : PAD + T * y + T, :]
        bits_ref[x, T * y : T * y + T, :] = (total * here).astype(jnp.int32)

    sweep_interior(mark)
    second = middle(post_1, post_2)
    sweep_interior(second)

    for load in seed_load:
        load.wait()
    sweep(0, nx, lambda x: pack_plane(4, held, x))
    pack_corners(4, held, SLOW)
    pack_corners(4, held, FAST)
    seed_rims = row_copies(4, Y_SLOW, pl.ds(0, nx)) + corner_copies(4, SLOW) + corner_copies(4, FAST)
    begin(seed_rims)
    begin(seed_faces[FAST])

    arrive(cell_copies)

    def place_cells(x):
        solid[x + 1, PAD - 1 : PAD, :] = y_recv[0, 0, x, 0]
        solid[x + 1, top : top + 1, :] = y_recv[0, 1, x, 0]

    sweep(0, nx, place_cells)
    for side in (SLOW, FAST):
        halo = halo_of(1 - sign[side])
        solid[halo, PAD - 1 : PAD, :] = c_recv[0, 2 * side]
        solid[halo, top : top + 1, :] = c_recv[0, 2 * side + 1]
    sweep_edges(mark)

    def mark_face(i):
        for y in range(tiles):
            mark(i * (nx - 1), y)

    sweep(0, 2, mark_face)

    take_rows(1, post_1, slow_1, fast_1)
    sweep_edges(second)
    take_fast(1, post_1, fast_1)
    fast_2 = send_fast(2, post_2, second)
    send_rows(2, post_2, fast_2)
    take_outer(1, post_1, slow_1)
    slow_2 = send_outer(2, post_2, second)
    arrive(slow_1["middle"])
    send_middle(2, slow_2, second)
    begin(seed_faces[SLOW][2:4])

    third = middle(post_2, post_3)
    sweep_interior(third)
    take_rows(2, post_2, slow_2, fast_2)
    sweep_edges(third)
    take_fast(2, post_2, fast_2)
    fast_3 = send_fast(3, post_3, third)
    send_rows(3, post_3, fast_3)
    take_outer(2, post_2, slow_2)
    slow_3 = send_outer(3, post_3, third)
    begin(seed_faces[SLOW][4:])

    def final(x, y):
        rows = slice(T * y, T * y + T)
        bits = bits_ref[x, rows, :]
        v = stream(post_3, bits, x, y)
        for q in range(19):
            state_ref[q, x, rows, :] = v[q]
        turned = stream(held, bits, x, y)
        through = pull_back(v, [turned[OPPOSITE[q]] for q in range(19)])
        is_fluid = (bits & 1) != 0
        for q in range(19):
            adjoint_ref[q, x, rows, :] = jnp.where(is_fluid, through[q], turned[q])

    arrive(slow_2["middle"])
    send_middle(3, slow_3, third)
    sweep_interior(final)
    arrive(seed_rims)
    sweep(0, nx, lambda x: unpack_plane(4, held, x))
    unpack_corners(4, held, SLOW)
    unpack_corners(4, held, FAST)
    take_rows(3, post_3, slow_3, fast_3)
    sweep_edges(final)
    take_fast(3, post_3, fast_3)
    arrive(seed_faces[FAST])
    for y in range(tiles):
        final(face[FAST], y)
    take_outer(3, post_3, slow_3)
    arrive(slow_3["middle"])
    arrive(seed_faces[SLOW])
    for y in range(tiles):
        final(face[SLOW], y)
    for copy in sent:
        copy.wait_send()


def write_kernel(state_in, adjoint_in, state_ref, adjoint_ref, sem):
    made = []
    for i, (source, target) in enumerate(((state_in, state_ref), (adjoint_in, adjoint_ref))):
        for q in range(source.shape[0]):
            made.append(pltpu.make_async_copy(source.at[q], target.at[q], sem.at[i, q]))
    for copy in made:
        copy.start()
    for copy in made:
        copy.wait()


def per_device(checkpoint, fluid, adjoint_in):
    n, nx, ny, nz = checkpoint.shape
    padded = (n, nx + 2, ny + 2 * PAD, nz)
    f32 = jnp.float32
    state, adjoint = pl.pallas_call(
        forward_kernel,
        out_shape=(
            pltpu.VMEM((n, nx, ny, nz), f32),
            pltpu.VMEM((n, nx, ny, nz), f32),
        ),
        in_specs=[pl.BlockSpec(memory_space=pltpu.HBM)] * 3,
        out_specs=[pl.BlockSpec(memory_space=pltpu.VMEM)] * 2,
        scratch_shapes=[
            pltpu.VMEM(padded, f32),
            pltpu.VMEM(padded, f32),
            pltpu.VMEM(padded, f32),
            pltpu.VMEM(padded, f32),
            pltpu.VMEM((nx, ny, nz), jnp.int32),
            pltpu.VMEM((n, nx, ny, nz), f32),
            pltpu.VMEM((nx, ny, nz), jnp.int32),
            pltpu.VMEM(padded[1:], f32),
            pltpu.VMEM((5, 2, nx, 5, 1, nz), f32),
            pltpu.VMEM((5, 2, nx, 5, 1, nz), f32),
            pltpu.VMEM((5, 4, 1, nz), f32),
            pltpu.VMEM((5, 4, 1, nz), f32),
            pltpu.SemaphoreType.DMA((23,)),
            pltpu.SemaphoreType.DMA((5, LANES)),
            pltpu.SemaphoreType.DMA((5, LANES)),
            pltpu.SemaphoreType.DMA((2, 5)),
            pltpu.SemaphoreType.DMA((2, 5)),
        ],
        compiler_params=pltpu.CompilerParams(
            collective_id=0, has_side_effects=True, vmem_limit_bytes=50 * MIB
        ),
        name="forward",
    )(checkpoint, fluid, adjoint_in)
    return pl.pallas_call(
        write_kernel,
        out_shape=(jax.ShapeDtypeStruct((n, nx, ny, nz), f32),) * 2,
        in_specs=[pl.BlockSpec(memory_space=pltpu.VMEM)] * 2,
        out_specs=[pl.BlockSpec(memory_space=pl.ANY)] * 2,
        scratch_shapes=[pltpu.SemaphoreType.DMA((2, n))],
        compiler_params=pltpu.CompilerParams(vmem_limit_bytes=4 * MIB),
        name="write",
    )(state, adjoint)


def solution(mesh):
    return jax.shard_map(
        per_device,
        mesh=mesh,
        in_specs=(P(None, "gx", "gy", None), P("gx", "gy", None), P(None, "gx", "gy", None)),
        out_specs=(P(None, "gx", "gy", None), P(None, "gx", "gy", None)),
        check_vma=False,
    )
```

```python
import jax
import jax.numpy as jnp
from jax import lax
from jax.experimental import pallas as pl
from jax.experimental.pallas import tpu as pltpu
from jax.sharding import PartitionSpec as P

VELOCITY = [
    (0, 0, 0),
    (1, 0, 0),
    (-1, 0, 0),
    (0, 1, 0),
    (0, -1, 0),
    (0, 0, 1),
    (0, 0, -1),
    (1, 1, 0),
    (-1, -1, 0),
    (1, -1, 0),
    (-1, 1, 0),
    (1, 0, 1),
    (-1, 0, -1),
    (1, 0, -1),
    (-1, 0, 1),
    (0, 1, 1),
    (0, -1, -1),
    (0, 1, -1),
    (0, -1, 1),
]
OPPOSITE = [0, 2, 1, 4, 3, 6, 5, 8, 7, 10, 9, 12, 11, 14, 13, 16, 15, 18, 17]
ORDER = [0, 1, 7, 9, 11, 13, 2, 8, 10, 12, 14, 3, 4, 5, 6, 15, 16, 17, 18]
SLOT = [ORDER.index(q) for q in range(19)]
UP = [3, 7, 10, 15, 17]
DOWN = [4, 8, 9, 16, 18]
CORNER = [7, 8, 9, 10]
PAD = 8
T = 8
MIB = 1 << 20


def shifted(ref, q, x, y, speed):
    row = PAD + T * y - speed[1]
    tile = ref[SLOT[q], x + 1 - speed[0], row : row + T, :]
    if speed[2]:
        tile = pltpu.roll(tile, speed[2] % tile.shape[1], 1)
    return tile


def own(ref, q, x, y):
    return ref[SLOT[q], x + 1, PAD + T * y : PAD + T * y + T, :]


def stream(ref, bits, x, y):
    result = [own(ref, 0, x, y)]
    for q in range(1, 19):
        is_open = (bits & (1 << q)) != 0
        result.append(
            jnp.where(is_open, shifted(ref, q, x, y, VELOCITY[q]), own(ref, OPPOSITE[q], x, y))
        )
    return result


def moments(v):
    s = {q: v[q] + v[q + 1] for q in range(1, 19, 2)}
    d = {q: v[q] - v[q + 1] for q in range(1, 19, 2)}
    rho = v[0] + ((s[1] + s[3]) + (s[5] + s[7])) + ((s[9] + s[11]) + (s[13] + (s[15] + s[17])))
    mx = d[1] + (d[7] + d[9]) + (d[11] + d[13])
    my = d[3] + (d[7] - d[9]) + (d[15] + d[17])
    mz = d[5] + (d[11] - d[13]) + (d[15] - d[17])
    return rho, mx, my, mz


def collide(v):
    rho, mx, my, mz = moments(v)
    inverse = 3.0 / rho
    ux, uy, uz = mx * inverse, my * inverse, mz * inverse
    base = 1.0 - (ux * ux + uy * uy + uz * uz) * (1.0 / 6.0)
    along = {
        1: ux,
        3: uy,
        5: uz,
        7: ux + uy,
        9: ux - uy,
        11: ux + uz,
        13: ux - uz,
        15: uy + uz,
        17: uy - uz,
    }
    axis, diagonal = rho * (1.6 / 18.0), rho * (1.6 / 36.0)
    result = [rho * (1.6 / 3.0) * base - 0.6 * v[0]]
    for q in range(1, 19, 2):
        a = along[q]
        even = base + 0.5 * (a * a)
        factor = axis if q < 7 else diagonal
        result.append(factor * (even + a) - 0.6 * v[q])
        result.append(factor * (even - a) - 0.6 * v[q + 1])
    return result


def pull_back(v, b):
    rho, mx, my, mz = moments(v)
    inverse = 1.0 / rho
    ux, uy, uz = mx * inverse, my * inverse, mz * inverse
    s = {q: b[q] + b[q + 1] for q in range(1, 19, 2)}
    d = {q: b[q] - b[q + 1] for q in range(1, 19, 2)}
    for q in (1, 3, 5):
        s[q] = s[q] + s[q]
        d[q] = d[q] + d[q]
    sxy_p, sxz_p, syz_p = s[7] + s[9], s[11] + s[13], s[15] + s[17]
    sxy, sxz, syz = s[7] - s[9], s[11] - s[13], s[15] - s[17]
    s0 = 12.0 * b[0] + (s[1] + s[3]) + (s[5] + sxy_p) + (sxz_p + syz_p)
    sxx, syy, szz = s[1] + sxy_p + sxz_p, s[3] + sxy_p + syz_p, s[5] + sxz_p + syz_p
    s1x = d[1] + (d[7] + d[9]) + (d[11] + d[13])
    s1y = d[3] + (d[7] - d[9]) + (d[15] + d[17])
    s1z = d[5] + (d[11] - d[13]) + (d[15] - d[17])
    tx = sxx * ux + sxy * uy + sxz * uz
    ty = sxy * ux + syy * uy + syz * uz
    tz = sxz * ux + syz * uy + szz * uz
    k = 1.6 / 36.0
    square = ux * ux + uy * uy + uz * uz
    level = k * (s0 * (1.0 + 1.5 * square) - 4.5 * (ux * tx + uy * ty + uz * tz))
    gx = (3.0 * k) * (s1x + 3.0 * tx - ux * s0)
    gy = (3.0 * k) * (s1y + 3.0 * ty - uy * s0)
    gz = (3.0 * k) * (s1z + 3.0 * tz - uz * s0)
    along = {
        1: gx,
        3: gy,
        5: gz,
        7: gx + gy,
        9: gx - gy,
        11: gx + gz,
        13: gx - gz,
        15: gy + gz,
        17: gy - gz,
    }
    result = [level - 0.6 * b[0]]
    for q in range(1, 19, 2):
        result.append((level + along[q]) - 0.6 * b[q])
        result.append((level - along[q]) - 0.6 * b[q + 1])
    return result


SLOW, FAST = 0, 1
OUTER, MIDDLE, OTHER, ROWS = 0, 1, 2, 3
CELLS_IN, SEEDS_IN, SEED_FACES_IN = 12, 13, 14
CELLS_OUT, SLOW_OUT, REST_OUT = 0, 1, 2


def forward_kernel(
    start_ref, fluid_ref, seed_ref,
    state_ref, adjoint_ref,
    post_1, post_2, post_3, held, bits_ref, start, cells, solid,
    y_send, y_recv,
    load_sem, send_sem, recv_sem,
):
    _, nx, ny, nz = start_ref.shape
    tiles = ny // T
    last = tiles - 1
    top = PAD + ny
    me = {"gx": lax.axis_index("gx"), "gy": lax.axis_index("gy")}
    count = {"gx": lax.axis_size("gx"), "gy": lax.axis_size("gy")}
    odd = lax.rem(me["gx"], 2)
    sign = {SLOW: odd, FAST: 1 - odd}
    face = {side: (nx - 1) * p for side, p in sign.items()}
    rest = pl.ds(1 - odd, nx - 1)

    def first_of(p):
        return 6 - 5 * p

    def corner_of(p, up):
        return 8 - 6 * p if up else 7 - 4 * p

    def halo_of(p):
        return (nx + 1) * (1 - p)

    def device(dx, dy):
        to_x = lax.rem(me["gx"] + dx + count["gx"], count["gx"])
        to_y = lax.rem(me["gy"] + dy + count["gy"], count["gy"])
        return (to_x, to_y)

    def toward(side, dy):
        return device(2 * sign[side] - 1, dy)

    around = [(i, j) for i in (-1, 0, 1) for j in (-1, 0, 1) if (i, j) != (0, 0)]
    barrier = pltpu.get_barrier_semaphore()
    for i, j in around:
        pl.semaphore_signal(barrier, inc=1, device_id=device(i, j), device_id_type=pl.DeviceIdType.MESH)

    fluid_load = pltpu.make_async_copy(fluid_ref, cells, load_sem.at[0])
    fluid_load.start()
    start_load = [
        pltpu.make_async_copy(start_ref.at[:, planes], start.at[:, planes], load_sem.at[1 + i])
        for i, planes in enumerate((pl.ds(face[SLOW], 1), pl.ds(face[FAST], 1), pl.ds(1, nx - 2)))
    ]
    for load in start_load:
        load.start()
    seed_load = [
        pltpu.make_async_copy(
            seed_ref.at[q],
            held.at[SLOT[OPPOSITE[q]], pl.ds(1, nx), pl.ds(PAD, ny)],
            load_sem.at[4],
        )
        for q in range(19)
    ]

    def wait_rows(rows, sem):
        part = next(c for c in range(ny + 2 * PAD, 0, -T) if rows % c == 0)
        outer = rows // part
        planes = next(c for c in range(nx + 2, 0, -1) if outer % c == 0)
        view = post_1.at[pl.ds(0, outer // planes), pl.ds(0, planes), pl.ds(0, part)]
        pltpu.make_async_copy(view, view, sem).wait()

    def remote(source, target, out, into, to):
        return pltpu.make_async_remote_copy(
            src_ref=source, dst_ref=target, send_sem=send_sem.at[out], recv_sem=recv_sem.at[into],
            device_id=to, device_id_type=pl.DeviceIdType.MESH,
        )

    def lane(e, kind):
        return 4 * (e - 1) + kind

    seed_faces = {
        side: [
            remote(
                seed_ref.at[2 * k + 5 + p if k else 1 + p, face[side]],
                held.at[first_of(p) + k, halo_of(p), pl.ds(PAD, ny)],
                SLOW_OUT if side == SLOW else REST_OUT,
                SEED_FACES_IN if side == SLOW else SEEDS_IN,
                toward(side, 0),
            )
            for k in range(5)
        ]
        for side, p in sign.items()
    }

    def face_copy(into, ref, side, first_tile, end_tile):
        p = sign[side]
        five, rows = pl.ds(first_of(p), 5), pl.ds(PAD + T * first_tile, T * (end_tile - first_tile))
        return remote(
            ref.at[five, face[side] + 1, rows], ref.at[five, halo_of(p), rows],
            SLOW_OUT if side == SLOW else REST_OUT, into, toward(side, 0),
        )

    def row_copies(e, into, planes):
        return [
            remote(y_send.at[e, i, planes], y_recv.at[e, i, planes], REST_OUT, into, device(0, 1 - 2 * i))
            for i in range(2)
        ]

    ends = ((pl.ds(top - T, T), pl.ds(PAD - T, T)), (pl.ds(PAD, T), pl.ds(top, T)))

    def corner_copies(into, ref, side):
        p = sign[side]
        return [
            remote(
                ref.at[corner_of(p, i == 0), face[side] + 1, source],
                ref.at[corner_of(p, i == 0), halo_of(p), target],
                REST_OUT, into, toward(side, 1 - 2 * i),
            )
            for i, (source, target) in enumerate(ends)
        ]

    def pack_plane(e, ref, x):
        for k in range(5):
            y_send[e, 0, x, k] = ref[SLOT[UP[k]], x + 1, top - 1 : top, :]
            y_send[e, 1, x, k] = ref[SLOT[DOWN[k]], x + 1, PAD : PAD + 1, :]

    def unpack_plane(e, ref, x):
        for k in range(5):
            ref[SLOT[UP[k]], x + 1, PAD - 1 : PAD, :] = y_recv[e, 0, x, k]
            ref[SLOT[DOWN[k]], x + 1, top : top + 1, :] = y_recv[e, 1, x, k]

    def sweep(begin_at, length, body):
        def one(i, _):
            body(begin_at + i)
            return 0

        lax.fori_loop(0, length, one, 0)

    def begin(made):
        for copy in made:
            copy.start()

    fluid_load.wait()

    def to_float(x):
        solid[x + 1, PAD:top, :] = cells[x].astype(jnp.float32)
        y_send[0, 0, x, 0] = solid[x + 1, top - 1 : top, :]
        y_send[0, 1, x, 0] = solid[x + 1, PAD : PAD + 1, :]

    sweep(0, nx, to_float)
    pl.semaphore_wait(barrier, len(around))
    cell_copies = [
        remote(
            solid.at[face[side] + 1, source], solid.at[halo_of(sign[side]), target],
            CELLS_OUT, CELLS_IN, toward(side, dy),
        )
        for side in (SLOW, FAST)
        for dy, (source, target) in zip((0, 1, -1), ((pl.ds(PAD, ny),) * 2,) + ends)
    ]
    cell_copies += [
        remote(y_send.at[0, i, :, 0], y_recv.at[0, i, :, 0], CELLS_OUT, CELLS_IN, device(0, 1 - 2 * i))
        for i in range(2)
    ]
    cell_rows = 2 * (ny + 2 * T + nx)
    begin(cell_copies)

    def store(to, x, y, v, is_fluid):
        for q, value in enumerate(collide(v)):
            to[SLOT[q], x + 1, PAD + T * y : PAD + T * y + T, :] = jnp.where(
                is_fluid, value, v[OPPOSITE[q]]
            )

    def first(x, y):
        v = [start[q, x, T * y : T * y + T, :] for q in range(19)]
        store(post_1, x, y, v, solid[x + 1, PAD + T * y : PAD + T * y + T, :] > 0.5)

    def middle(source, to):
        def body(x, y):
            bits = bits_ref[x, T * y : T * y + T, :]
            v = stream(source, bits, x, y)
            store(to, x, y, v, (bits & 1) != 0)

        return body

    def edge_line(body):
        def line(x):
            body(x, 0)
            body(x, last)

        return line

    def inner_line(body):
        def line(x):
            for y in range(1, last):
                body(x, y)

        return line

    def sweep_edges(body):
        sweep(1, nx - 2, edge_line(body))

    def sweep_interior(body):
        sweep(1, nx - 2, inner_line(body))

    def send_outer(e, to, body):
        outer = 4 - e
        into = lane(e, OUTER)
        for i in range(outer):
            body(face[SLOW], i)
            body(face[SLOW], last - i)
            if i == 0:
                begin(corner_copies(into, to, SLOW))
                pack_plane(e, to, face[SLOW])
                begin(row_copies(e, lane(e, ROWS), pl.ds(face[SLOW], 1)))
        begin([face_copy(into, to, SLOW, 0, outer), face_copy(into, to, SLOW, tiles - outer, tiles)])

    def take_outer(e):
        wait_rows(2 * T * (5 * (4 - e) + 1), recv_sem.at[lane(e, OUTER)])

    def send_middle(e, to, body):
        outer = 4 - e
        for y in range(outer, tiles - outer):
            body(face[SLOW], y)
        begin([face_copy(lane(e, MIDDLE), to, SLOW, outer, tiles - outer)])

    def take_middle(e):
        wait_rows(5 * T * (tiles - 2 * (4 - e)), recv_sem.at[lane(e, MIDDLE)])

    def send_fast(e, to, body):
        for y in range(tiles):
            body(face[FAST], y)
        into = lane(e, OTHER)
        begin(corner_copies(into, to, FAST))
        begin([face_copy(into, to, FAST, 0, tiles)])

    def take_fast(e):
        wait_rows(5 * ny + 2 * T, recv_sem.at[lane(e, OTHER)])

    def send_rows(e, to):
        sweep(1 - odd, nx - 1, lambda x: pack_plane(e, to, x))
        begin(row_copies(e, lane(e, ROWS), rest))

    def take_rows(e, ref):
        wait_rows(10 * nx, recv_sem.at[lane(e, ROWS)])
        sweep(0, nx, lambda x: unpack_plane(e, ref, x))

    start_load[0].wait()
    send_outer(1, post_1, first)
    send_middle(1, post_1, first)
    begin(seed_faces[SLOW][:2])
    start_load[1].wait()
    send_fast(1, post_1, first)
    start_load[2].wait()
    for load in seed_load:
        load.start()
    sweep_edges(first)
    send_rows(1, post_1)
    sweep_interior(first)

    layer = lax.broadcasted_iota(jnp.int32, (T, nz), 1)
    inside = {1: (layer > 0).astype(jnp.float32), -1: (layer < nz - 1).astype(jnp.float32)}

    def mark(x, y):
        flat, up, down = 1.0, 0.0, 0.0
        for q in range(1, 19):
            c = VELOCITY[q]
            row = PAD + T * y - c[1]
            tile = solid[x + 1 - c[0], row : row + T, :] * float(1 << q)
            if c[2] == 0:
                flat = flat + tile
            elif c[2] == 1:
                up = up + tile
            else:
                down = down + tile
        total = flat + pltpu.roll(up, 1, 1) * inside[1] + pltpu.roll(down, nz - 1, 1) * inside[-1]
        here = solid[x + 1, PAD + T * y : PAD + T * y + T, :]
        bits_ref[x, T * y : T * y + T, :] = (total * here).astype(jnp.int32)

    sweep_interior(mark)
    second = middle(post_1, post_2)
    sweep_interior(second)

    wait_rows(19 * nx * ny, load_sem.at[4])
    sweep(0, nx, lambda x: pack_plane(4, held, x))
    begin(row_copies(4, SEEDS_IN, pl.ds(0, nx)))
    begin(corner_copies(SEEDS_IN, held, SLOW) + corner_copies(SEEDS_IN, held, FAST))
    begin(seed_faces[FAST])

    wait_rows(cell_rows, recv_sem.at[CELLS_IN])

    def place_cells(x):
        solid[x + 1, PAD - 1 : PAD, :] = y_recv[0, 0, x, 0]
        solid[x + 1, top : top + 1, :] = y_recv[0, 1, x, 0]

    sweep(0, nx, place_cells)
    sweep_edges(mark)

    def mark_face(i):
        for y in range(tiles):
            mark(i * (nx - 1), y)

    sweep(0, 2, mark_face)

    take_rows(1, post_1)
    sweep_edges(second)
    take_fast(1)
    send_fast(2, post_2, second)
    send_rows(2, post_2)
    take_outer(1)
    send_outer(2, post_2, second)
    take_middle(1)
    send_middle(2, post_2, second)
    begin(seed_faces[SLOW][2:4])

    third = middle(post_2, post_3)
    sweep_interior(third)
    take_rows(2, post_2)
    sweep_edges(third)
    take_fast(2)
    send_fast(3, post_3, third)
    send_rows(3, post_3)
    take_outer(2)
    send_outer(3, post_3, third)
    begin(seed_faces[SLOW][4:])

    def final(x, y):
        rows = slice(T * y, T * y + T)
        bits = bits_ref[x, rows, :]
        v = stream(post_3, bits, x, y)
        for q in range(19):
            state_ref[q, x, rows, :] = v[q]
        turned = stream(held, bits, x, y)
        through = pull_back(v, [turned[OPPOSITE[q]] for q in range(19)])
        is_fluid = (bits & 1) != 0
        for q in range(19):
            adjoint_ref[q, x, rows, :] = jnp.where(is_fluid, through[q], turned[q])

    take_middle(2)
    send_middle(3, post_3, third)
    sweep_interior(final)
    wait_rows(5 * ny + 10 * nx + 4 * T, recv_sem.at[SEEDS_IN])
    sweep(0, nx, lambda x: unpack_plane(4, held, x))
    take_rows(3, post_3)
    sweep_edges(final)
    take_fast(3)
    for y in range(tiles):
        final(face[FAST], y)
    take_outer(3)
    take_middle(3)
    wait_rows(5 * ny, recv_sem.at[SEED_FACES_IN])
    for y in range(tiles):
        final(face[SLOW], y)
    wait_rows(cell_rows, send_sem.at[CELLS_OUT])
    wait_rows(4 * 5 * ny, send_sem.at[SLOW_OUT])
    wait_rows(4 * (5 * ny + 10 * nx + 4 * T), send_sem.at[REST_OUT])


def write_kernel(state_in, adjoint_in, state_ref, adjoint_ref, sem):
    pairs = ((state_in, state_ref), (adjoint_in, adjoint_ref))
    made = [pltpu.make_async_copy(source, target, sem.at[i]) for i, (source, target) in enumerate(pairs)]
    for copy in made:
        copy.start()
    for copy in made:
        copy.wait()


def per_device(checkpoint, fluid, adjoint_in):
    n, nx, ny, nz = checkpoint.shape
    padded = (n, nx + 2, ny + 2 * PAD, nz)
    f32 = jnp.float32
    state, adjoint = pl.pallas_call(
        forward_kernel,
        out_shape=(
            pltpu.VMEM((n, nx, ny, nz), f32),
            pltpu.VMEM((n, nx, ny, nz), f32),
        ),
        in_specs=[pl.BlockSpec(memory_space=pltpu.HBM)] * 3,
        out_specs=[pl.BlockSpec(memory_space=pltpu.VMEM)] * 2,
        scratch_shapes=[
            pltpu.VMEM(padded, f32),
            pltpu.VMEM(padded, f32),
            pltpu.VMEM(padded, f32),
            pltpu.VMEM(padded, f32),
            pltpu.VMEM((nx, ny, nz), jnp.int32),
            pltpu.VMEM((n, nx, ny, nz), f32),
            pltpu.VMEM((nx, ny, nz), jnp.int32),
            pltpu.VMEM(padded[1:], f32),
            pltpu.VMEM((5, 2, nx, 5, 1, nz), f32),
            pltpu.VMEM((5, 2, nx, 5, 1, nz), f32),
            pltpu.SemaphoreType.DMA((5,)),
            pltpu.SemaphoreType.DMA((3,)),
            pltpu.SemaphoreType.DMA((15,)),
        ],
        compiler_params=pltpu.CompilerParams(
            collective_id=0, has_side_effects=True, vmem_limit_bytes=50 * MIB
        ),
        name="forward",
    )(checkpoint, fluid, adjoint_in)
    return pl.pallas_call(
        write_kernel,
        out_shape=(jax.ShapeDtypeStruct((n, nx, ny, nz), f32),) * 2,
        in_specs=[pl.BlockSpec(memory_space=pltpu.VMEM)] * 2,
        out_specs=[pl.BlockSpec(memory_space=pl.ANY)] * 2,
        scratch_shapes=[pltpu.SemaphoreType.DMA((2,))],
        compiler_params=pltpu.CompilerParams(vmem_limit_bytes=4 * MIB),
        name="write",
    )(state, adjoint)


def solution(mesh):
    return jax.shard_map(
        per_device,
        mesh=mesh,
        in_specs=(P(None, "gx", "gy", None), P("gx", "gy", None), P(None, "gx", "gy", None)),
        out_specs=(P(None, "gx", "gy", None), P(None, "gx", "gy", None)),
        check_vma=False,
    )
```

```python
import jax
import jax.numpy as jnp
from jax import lax
from jax.experimental import pallas as pl
from jax.experimental.pallas import tpu as pltpu
from jax.sharding import PartitionSpec as P

VELOCITY = [
    (0, 0, 0),
    (1, 0, 0),
    (-1, 0, 0),
    (0, 1, 0),
    (0, -1, 0),
    (0, 0, 1),
    (0, 0, -1),
    (1, 1, 0),
    (-1, -1, 0),
    (1, -1, 0),
    (-1, 1, 0),
    (1, 0, 1),
    (-1, 0, -1),
    (1, 0, -1),
    (-1, 0, 1),
    (0, 1, 1),
    (0, -1, -1),
    (0, 1, -1),
    (0, -1, 1),
]
OPPOSITE = [0, 2, 1, 4, 3, 6, 5, 8, 7, 10, 9, 12, 11, 14, 13, 16, 15, 18, 17]
ORDER = [0, 1, 7, 9, 11, 13, 2, 8, 10, 12, 14, 3, 4, 5, 6, 15, 16, 17, 18]
SLOT = [ORDER.index(q) for q in range(19)]
UP = [3, 7, 10, 15, 17]
DOWN = [4, 8, 9, 16, 18]
CORNER = [7, 8, 9, 10]
PAD = 8
T = 8
MIB = 1 << 20


def shifted(ref, q, x, y, speed):
    row = PAD + T * y - speed[1]
    tile = ref[SLOT[q], x + 1 - speed[0], row : row + T, :]
    if speed[2]:
        tile = pltpu.roll(tile, speed[2] % tile.shape[1], 1)
    return tile


def own(ref, q, x, y):
    return ref[SLOT[q], x + 1, PAD + T * y : PAD + T * y + T, :]


def stream(ref, bits, x, y):
    result = [own(ref, 0, x, y)]
    for q in range(1, 19):
        is_open = (bits & (1 << q)) != 0
        result.append(
            jnp.where(is_open, shifted(ref, q, x, y, VELOCITY[q]), own(ref, OPPOSITE[q], x, y))
        )
    return result


def moments(v):
    s = {q: v[q] + v[q + 1] for q in range(1, 19, 2)}
    d = {q: v[q] - v[q + 1] for q in range(1, 19, 2)}
    rho = v[0] + ((s[1] + s[3]) + (s[5] + s[7])) + ((s[9] + s[11]) + (s[13] + (s[15] + s[17])))
    mx = d[1] + (d[7] + d[9]) + (d[11] + d[13])
    my = d[3] + (d[7] - d[9]) + (d[15] + d[17])
    mz = d[5] + (d[11] - d[13]) + (d[15] - d[17])
    return rho, mx, my, mz


def collide(v):
    rho, mx, my, mz = moments(v)
    inverse = 3.0 / rho
    ux, uy, uz = mx * inverse, my * inverse, mz * inverse
    base = 1.0 - (ux * ux + uy * uy + uz * uz) * (1.0 / 6.0)
    along = {
        1: ux,
        3: uy,
        5: uz,
        7: ux + uy,
        9: ux - uy,
        11: ux + uz,
        13: ux - uz,
        15: uy + uz,
        17: uy - uz,
    }
    axis, diagonal = rho * (1.6 / 18.0), rho * (1.6 / 36.0)
    result = [rho * (1.6 / 3.0) * base - 0.6 * v[0]]
    for q in range(1, 19, 2):
        a = along[q]
        even = base + 0.5 * (a * a)
        factor = axis if q < 7 else diagonal
        result.append(factor * (even + a) - 0.6 * v[q])
        result.append(factor * (even - a) - 0.6 * v[q + 1])
    return result


def pull_back(v, b):
    rho, mx, my, mz = moments(v)
    inverse = 1.0 / rho
    ux, uy, uz = mx * inverse, my * inverse, mz * inverse
    s = {q: b[q] + b[q + 1] for q in range(1, 19, 2)}
    d = {q: b[q] - b[q + 1] for q in range(1, 19, 2)}
    for q in (1, 3, 5):
        s[q] = s[q] + s[q]
        d[q] = d[q] + d[q]
    sxy_p, sxz_p, syz_p = s[7] + s[9], s[11] + s[13], s[15] + s[17]
    sxy, sxz, syz = s[7] - s[9], s[11] - s[13], s[15] - s[17]
    s0 = 12.0 * b[0] + (s[1] + s[3]) + (s[5] + sxy_p) + (sxz_p + syz_p)
    sxx, syy, szz = s[1] + sxy_p + sxz_p, s[3] + sxy_p + syz_p, s[5] + sxz_p + syz_p
    s1x = d[1] + (d[7] + d[9]) + (d[11] + d[13])
    s1y = d[3] + (d[7] - d[9]) + (d[15] + d[17])
    s1z = d[5] + (d[11] - d[13]) + (d[15] - d[17])
    tx = sxx * ux + sxy * uy + sxz * uz
    ty = sxy * ux + syy * uy + syz * uz
    tz = sxz * ux + syz * uy + szz * uz
    k = 1.6 / 36.0
    square = ux * ux + uy * uy + uz * uz
    level = k * (s0 * (1.0 + 1.5 * square) - 4.5 * (ux * tx + uy * ty + uz * tz))
    gx = (3.0 * k) * (s1x + 3.0 * tx - ux * s0)
    gy = (3.0 * k) * (s1y + 3.0 * ty - uy * s0)
    gz = (3.0 * k) * (s1z + 3.0 * tz - uz * s0)
    along = {
        1: gx,
        3: gy,
        5: gz,
        7: gx + gy,
        9: gx - gy,
        11: gx + gz,
        13: gx - gz,
        15: gy + gz,
        17: gy - gz,
    }
    result = [level - 0.6 * b[0]]
    for q in range(1, 19, 2):
        result.append((level + along[q]) - 0.6 * b[q])
        result.append((level - along[q]) - 0.6 * b[q + 1])
    return result


SLOW, FAST = 0, 1
OUTER, MIDDLE, OTHER, ROWS = 0, 1, 2, 3
CELLS_IN, SEEDS_IN, SEED_FACES_IN = 12, 13, 14
CELLS_OUT, SLOW_OUT, REST_OUT = 0, 1, 2


def forward_kernel(
    start_ref, fluid_ref, seed_ref,
    state_ref, adjoint_ref,
    post_1, post_2, post_3, held, bits_ref, start, cells, solid,
    y_send, y_recv,
    load_sem, send_sem, recv_sem,
):
    _, nx, ny, nz = start_ref.shape
    tiles = ny // T
    last = tiles - 1
    top = PAD + ny
    me = {"gx": lax.axis_index("gx"), "gy": lax.axis_index("gy")}
    count = {"gx": lax.axis_size("gx"), "gy": lax.axis_size("gy")}
    odd = lax.rem(me["gx"], 2)
    sign = {SLOW: odd, FAST: 1 - odd}
    face = {side: (nx - 1) * p for side, p in sign.items()}
    rest = pl.ds(1 - odd, nx - 1)

    def first_of(p):
        return 6 - 5 * p

    def corner_of(p, up):
        return 8 - 6 * p if up else 7 - 4 * p

    def halo_of(p):
        return (nx + 1) * (1 - p)

    def device(dx, dy):
        to_x = lax.rem(me["gx"] + dx + count["gx"], count["gx"])
        to_y = lax.rem(me["gy"] + dy + count["gy"], count["gy"])
        return (to_x, to_y)

    def toward(side, dy):
        return device(2 * sign[side] - 1, dy)

    around = [(i, j) for i in (-1, 0, 1) for j in (-1, 0, 1) if (i, j) != (0, 0)]
    barrier = pltpu.get_barrier_semaphore()
    for i, j in around:
        pl.semaphore_signal(barrier, inc=1, device_id=device(i, j), device_id_type=pl.DeviceIdType.MESH)

    fluid_load = pltpu.make_async_copy(fluid_ref, cells, load_sem.at[0])
    fluid_load.start()
    slow_plane, fast_plane = pl.ds(face[SLOW], 1), pl.ds(face[FAST], 1)
    inner = pl.ds(1, nx - 2)
    start_load = [
        pltpu.make_async_copy(start_ref.at[:, planes, rows], start.at[:, planes, rows], load_sem.at[i])
        for i, planes, rows in (
            (1, slow_plane, pl.ds(0, ny)),
            (2, inner, pl.ds(0, T)),
            (2, inner, pl.ds(ny - T, T)),
            (2, fast_plane, pl.ds(0, ny)),
            (3, inner, pl.ds(T, ny - 2 * T)),
        )
    ]
    for load in start_load:
        load.start()
    seed_load = [
        pltpu.make_async_copy(
            seed_ref.at[q],
            held.at[SLOT[OPPOSITE[q]], pl.ds(1, nx), pl.ds(PAD, ny)],
            load_sem.at[4],
        )
        for q in range(19)
    ]

    def wait_rows(rows, sem):
        part, planes = next(
            (c, d)
            for c in range(ny + 2 * PAD, 0, -T)
            for d in range(nx + 2, 0, -1)
            if rows % (c * d) == 0 and rows <= 19 * c * d
        )
        view = post_1.at[pl.ds(0, rows // (part * planes)), pl.ds(0, planes), pl.ds(0, part)]
        pltpu.make_async_copy(view, view, sem).wait()

    def remote(source, target, out, into, to):
        return pltpu.make_async_remote_copy(
            src_ref=source, dst_ref=target, send_sem=send_sem.at[out], recv_sem=recv_sem.at[into],
            device_id=to, device_id_type=pl.DeviceIdType.MESH,
        )

    def lane(e, kind):
        return 4 * (e - 1) + kind

    seed_faces = {
        side: [
            remote(
                seed_ref.at[2 * k + 5 + p if k else 1 + p, face[side]],
                held.at[first_of(p) + k, halo_of(p), pl.ds(PAD, ny)],
                SLOW_OUT if side == SLOW else REST_OUT,
                SEED_FACES_IN if side == SLOW else SEEDS_IN,
                toward(side, 0),
            )
            for k in range(5)
        ]
        for side, p in sign.items()
    }

    def face_copy(into, ref, side, first_tile, end_tile):
        p = sign[side]
        five, rows = pl.ds(first_of(p), 5), pl.ds(PAD + T * first_tile, T * (end_tile - first_tile))
        return remote(
            ref.at[five, face[side] + 1, rows], ref.at[five, halo_of(p), rows],
            SLOW_OUT if side == SLOW else REST_OUT, into, toward(side, 0),
        )

    def row_copies(e, into, planes):
        return [
            remote(y_send.at[e, i, planes], y_recv.at[e, i, planes], REST_OUT, into, device(0, 1 - 2 * i))
            for i in range(2)
        ]

    ends = ((pl.ds(top - T, T), pl.ds(PAD - T, T)), (pl.ds(PAD, T), pl.ds(top, T)))

    def corner_copies(into, ref, side):
        p = sign[side]
        return [
            remote(
                ref.at[corner_of(p, i == 0), face[side] + 1, source],
                ref.at[corner_of(p, i == 0), halo_of(p), target],
                REST_OUT, into, toward(side, 1 - 2 * i),
            )
            for i, (source, target) in enumerate(ends)
        ]

    def pack_plane(e, ref, x):
        for k in range(5):
            y_send[e, 0, x, k] = ref[SLOT[UP[k]], x + 1, top - 1 : top, :]
            y_send[e, 1, x, k] = ref[SLOT[DOWN[k]], x + 1, PAD : PAD + 1, :]

    def unpack_plane(e, ref, x):
        for k in range(5):
            ref[SLOT[UP[k]], x + 1, PAD - 1 : PAD, :] = y_recv[e, 0, x, k]
            ref[SLOT[DOWN[k]], x + 1, top : top + 1, :] = y_recv[e, 1, x, k]

    def sweep(begin_at, length, body, unroll=True):
        def one(i, _):
            body(begin_at + i)
            return 0

        lax.fori_loop(0, length, one, 0, unroll=unroll)

    def begin(made):
        for copy in made:
            copy.start()

    fluid_load.wait()

    def to_float(x):
        solid[x + 1, PAD:top, :] = cells[x].astype(jnp.float32)
        y_send[0, 0, x, 0] = solid[x + 1, top - 1 : top, :]
        y_send[0, 1, x, 0] = solid[x + 1, PAD : PAD + 1, :]

    sweep(0, nx, to_float)
    pl.semaphore_wait(barrier, len(around))
    cell_copies = [
        remote(
            solid.at[face[side] + 1, source], solid.at[halo_of(sign[side]), target],
            CELLS_OUT, CELLS_IN, toward(side, dy),
        )
        for side in (SLOW, FAST)
        for dy, (source, target) in zip((0, 1, -1), ((pl.ds(PAD, ny),) * 2,) + ends)
    ]
    cell_copies += [
        remote(y_send.at[0, i, :, 0], y_recv.at[0, i, :, 0], CELLS_OUT, CELLS_IN, device(0, 1 - 2 * i))
        for i in range(2)
    ]
    cell_rows = 2 * (ny + 2 * T + nx)
    begin(cell_copies)

    def store(to, x, y, v, is_fluid):
        for q, value in enumerate(collide(v)):
            to[SLOT[q], x + 1, PAD + T * y : PAD + T * y + T, :] = jnp.where(
                is_fluid, value, v[OPPOSITE[q]]
            )

    def first(x, y):
        v = [start[q, x, T * y : T * y + T, :] for q in range(19)]
        store(post_1, x, y, v, solid[x + 1, PAD + T * y : PAD + T * y + T, :] > 0.5)

    def middle(source, to):
        def body(x, y):
            bits = bits_ref[x, T * y : T * y + T, :]
            v = stream(source, bits, x, y)
            store(to, x, y, v, (bits & 1) != 0)

        return body

    def edge_line(body):
        def line(x):
            body(x, 0)
            body(x, last)

        return line

    def inner_line(body):
        def line(x):
            for y in range(1, last):
                body(x, y)

        return line

    def sweep_edges(body):
        sweep(1 - odd, nx - 1, edge_line(body))

    def sweep_interior(body):
        sweep(1, nx - 2, inner_line(body), 1)

    def send_outer(e, to, body):
        outer = 4 - e
        into = lane(e, OUTER)
        for i in range(outer):
            body(face[SLOW], i)
            body(face[SLOW], last - i)
            if i == 0:
                begin(corner_copies(into, to, SLOW))
                pack_plane(e, to, face[SLOW])
                begin(row_copies(e, lane(e, ROWS), pl.ds(face[SLOW], 1)))
        begin([face_copy(into, to, SLOW, 0, outer), face_copy(into, to, SLOW, tiles - outer, tiles)])

    def take_outer(e):
        wait_rows(2 * T * (5 * (4 - e) + 1), recv_sem.at[lane(e, OUTER)])

    def send_middle(e, to, body):
        outer = 4 - e
        for y in range(outer, tiles - outer):
            body(face[SLOW], y)
        begin([face_copy(lane(e, MIDDLE), to, SLOW, outer, tiles - outer)])

    def take_middle(e):
        wait_rows(5 * T * (tiles - 2 * (4 - e)), recv_sem.at[lane(e, MIDDLE)])

    def send_edges(e, to, body):
        sweep_edges(body)
        begin(corner_copies(lane(e, OTHER), to, FAST))
        sweep(1 - odd, nx - 1, lambda x: pack_plane(e, to, x))
        begin(row_copies(e, lane(e, ROWS), rest))

    def send_fast(e, to, body):
        for y in range(1, last):
            body(face[FAST], y)
        begin([face_copy(lane(e, OTHER), to, FAST, 0, tiles)])

    def take_fast(e):
        wait_rows(5 * ny + 2 * T, recv_sem.at[lane(e, OTHER)])

    def take_rows(e, ref):
        wait_rows(10 * nx, recv_sem.at[lane(e, ROWS)])
        sweep(0, nx, lambda x: unpack_plane(e, ref, x))

    start_load[0].wait()
    send_outer(1, post_1, first)
    send_middle(1, post_1, first)
    begin(seed_faces[SLOW][:3])
    wait_rows(19 * (2 * T * (nx - 2) + ny), load_sem.at[2])
    send_edges(1, post_1, first)
    send_fast(1, post_1, first)
    wait_rows(19 * (nx - 2) * (ny - 2 * T), load_sem.at[3])
    for load in seed_load:
        load.start()
    sweep_interior(first)

    layer = lax.broadcasted_iota(jnp.int32, (T, nz), 1)
    inside = {1: (layer > 0).astype(jnp.float32), -1: (layer < nz - 1).astype(jnp.float32)}

    def mark(x, y):
        flat, up, down = 1.0, 0.0, 0.0
        for q in range(1, 19):
            c = VELOCITY[q]
            row = PAD + T * y - c[1]
            tile = solid[x + 1 - c[0], row : row + T, :] * float(1 << q)
            if c[2] == 0:
                flat = flat + tile
            elif c[2] == 1:
                up = up + tile
            else:
                down = down + tile
        total = flat + pltpu.roll(up, 1, 1) * inside[1] + pltpu.roll(down, nz - 1, 1) * inside[-1]
        here = solid[x + 1, PAD + T * y : PAD + T * y + T, :]
        bits_ref[x, T * y : T * y + T, :] = (total * here).astype(jnp.int32)

    sweep_interior(mark)
    second = middle(post_1, post_2)
    sweep_interior(second)

    wait_rows(19 * nx * ny, load_sem.at[4])
    sweep(0, nx, lambda x: pack_plane(4, held, x))
    begin(row_copies(4, SEEDS_IN, pl.ds(0, nx)))
    begin(corner_copies(SEEDS_IN, held, SLOW) + corner_copies(SEEDS_IN, held, FAST))
    begin(seed_faces[FAST])

    wait_rows(cell_rows, recv_sem.at[CELLS_IN])

    def place_cells(x):
        solid[x + 1, PAD - 1 : PAD, :] = y_recv[0, 0, x, 0]
        solid[x + 1, top : top + 1, :] = y_recv[0, 1, x, 0]

    sweep(0, nx, place_cells)
    sweep(0, nx, edge_line(mark))
    sweep(0, 2, lambda i: inner_line(mark)(i * (nx - 1)))

    take_rows(1, post_1)
    take_fast(1)
    send_edges(2, post_2, second)
    send_fast(2, post_2, second)
    take_outer(1)
    send_outer(2, post_2, second)
    take_middle(1)
    send_middle(2, post_2, second)
    begin(seed_faces[SLOW][3:4])

    third = middle(post_2, post_3)
    sweep_interior(third)
    take_rows(2, post_2)
    take_fast(2)
    send_edges(3, post_3, third)
    send_fast(3, post_3, third)
    take_outer(2)
    send_outer(3, post_3, third)
    begin(seed_faces[SLOW][4:])

    def final(x, y):
        rows = slice(T * y, T * y + T)
        bits = bits_ref[x, rows, :]
        v = stream(post_3, bits, x, y)
        for q in range(19):
            state_ref[q, x, rows, :] = v[q]
        turned = stream(held, bits, x, y)
        through = pull_back(v, [turned[OPPOSITE[q]] for q in range(19)])
        is_fluid = (bits & 1) != 0
        for q in range(19):
            adjoint_ref[q, x, rows, :] = jnp.where(is_fluid, through[q], turned[q])

    take_middle(2)
    send_middle(3, post_3, third)
    sweep_interior(final)
    wait_rows(5 * ny + 10 * nx + 4 * T, recv_sem.at[SEEDS_IN])
    sweep(0, nx, lambda x: unpack_plane(4, held, x))
    take_rows(3, post_3)
    take_fast(3)
    sweep_edges(final)
    for y in range(1, last):
        final(face[FAST], y)
    take_outer(3)
    take_middle(3)
    wait_rows(5 * ny, recv_sem.at[SEED_FACES_IN])
    for y in range(tiles):
        final(face[SLOW], y)
    wait_rows(cell_rows, send_sem.at[CELLS_OUT])
    wait_rows(4 * 5 * ny, send_sem.at[SLOW_OUT])
    wait_rows(4 * (5 * ny + 10 * nx + 4 * T), send_sem.at[REST_OUT])


def write_kernel(state_in, adjoint_in, state_ref, adjoint_ref, sem):
    pairs = ((state_in, state_ref), (adjoint_in, adjoint_ref))
    for i, (source, target) in enumerate(pairs):
        for q in range(source.shape[0]):
            pltpu.make_async_copy(source.at[q], target.at[q], sem.at[i]).start()
    for i, (source, target) in enumerate(pairs):
        pltpu.make_async_copy(source, target, sem.at[i]).wait()


def per_device(checkpoint, fluid, adjoint_in):
    n, nx, ny, nz = checkpoint.shape
    padded = (n, nx + 2, ny + 2 * PAD, nz)
    f32 = jnp.float32
    state, adjoint = pl.pallas_call(
        forward_kernel,
        out_shape=(
            pltpu.VMEM((n, nx, ny, nz), f32),
            pltpu.VMEM((n, nx, ny, nz), f32),
        ),
        in_specs=[pl.BlockSpec(memory_space=pltpu.HBM)] * 3,
        out_specs=[pl.BlockSpec(memory_space=pltpu.VMEM)] * 2,
        scratch_shapes=[
            pltpu.VMEM(padded, f32),
            pltpu.VMEM(padded, f32),
            pltpu.VMEM(padded, f32),
            pltpu.VMEM(padded, f32),
            pltpu.VMEM((nx, ny, nz), jnp.int32),
            pltpu.VMEM((n, nx, ny, nz), f32),
            pltpu.VMEM((nx, ny, nz), jnp.int32),
            pltpu.VMEM(padded[1:], f32),
            pltpu.VMEM((5, 2, nx, 5, 1, nz), f32),
            pltpu.VMEM((5, 2, nx, 5, 1, nz), f32),
            pltpu.SemaphoreType.DMA((5,)),
            pltpu.SemaphoreType.DMA((3,)),
            pltpu.SemaphoreType.DMA((15,)),
        ],
        compiler_params=pltpu.CompilerParams(
            collective_id=0, has_side_effects=True, vmem_limit_bytes=50 * MIB
        ),
        name="forward",
    )(checkpoint, fluid, adjoint_in)
    return pl.pallas_call(
        write_kernel,
        out_shape=(jax.ShapeDtypeStruct((n, nx, ny, nz), f32),) * 2,
        in_specs=[pl.BlockSpec(memory_space=pltpu.VMEM)] * 2,
        out_specs=[pl.BlockSpec(memory_space=pl.ANY)] * 2,
        scratch_shapes=[pltpu.SemaphoreType.DMA((2,))],
        compiler_params=pltpu.CompilerParams(vmem_limit_bytes=4 * MIB),
        name="write",
    )(state, adjoint)


def solution(mesh):
    return jax.shard_map(
        per_device,
        mesh=mesh,
        in_specs=(P(None, "gx", "gy", None), P("gx", "gy", None), P(None, "gx", "gy", None)),
        out_specs=(P(None, "gx", "gy", None), P(None, "gx", "gy", None)),
        check_vma=False,
    )
```

```python
import jax
import jax.numpy as jnp
from jax import lax
from jax.experimental import pallas as pl
from jax.experimental.pallas import tpu as pltpu
from jax.sharding import PartitionSpec as P

VELOCITY = [
    (0, 0, 0),
    (1, 0, 0),
    (-1, 0, 0),
    (0, 1, 0),
    (0, -1, 0),
    (0, 0, 1),
    (0, 0, -1),
    (1, 1, 0),
    (-1, -1, 0),
    (1, -1, 0),
    (-1, 1, 0),
    (1, 0, 1),
    (-1, 0, -1),
    (1, 0, -1),
    (-1, 0, 1),
    (0, 1, 1),
    (0, -1, -1),
    (0, 1, -1),
    (0, -1, 1),
]
OPPOSITE = [0, 2, 1, 4, 3, 6, 5, 8, 7, 10, 9, 12, 11, 14, 13, 16, 15, 18, 17]
ORDER = [0, 1, 7, 9, 11, 13, 2, 8, 10, 12, 14, 3, 4, 5, 6, 15, 16, 17, 18]
SLOT = [ORDER.index(q) for q in range(19)]
UP = [3, 7, 10, 15, 17]
DOWN = [4, 8, 9, 16, 18]
CORNER = [7, 8, 9, 10]
PAD = 8
T = 8
MIB = 1 << 20


def shifted(ref, q, x, y, speed):
    row = PAD + T * y - speed[1]
    tile = ref[SLOT[q], x + 1 - speed[0], row : row + T, :]
    if speed[2]:
        tile = pltpu.roll(tile, speed[2] % tile.shape[1], 1)
    return tile


def own(ref, q, x, y):
    return ref[SLOT[q], x + 1, PAD + T * y : PAD + T * y + T, :]


def stream(ref, bits, x, y):
    result = [own(ref, 0, x, y)]
    for q in range(1, 19):
        is_open = (bits & (1 << q)) != 0
        result.append(
            jnp.where(is_open, shifted(ref, q, x, y, VELOCITY[q]), own(ref, OPPOSITE[q], x, y))
        )
    return result


def moments(v):
    s = {q: v[q] + v[q + 1] for q in range(1, 19, 2)}
    d = {q: v[q] - v[q + 1] for q in range(1, 19, 2)}
    rho = v[0] + ((s[1] + s[3]) + (s[5] + s[7])) + ((s[9] + s[11]) + (s[13] + (s[15] + s[17])))
    mx = d[1] + (d[7] + d[9]) + (d[11] + d[13])
    my = d[3] + (d[7] - d[9]) + (d[15] + d[17])
    mz = d[5] + (d[11] - d[13]) + (d[15] - d[17])
    return rho, mx, my, mz


def collide(v):
    rho, mx, my, mz = moments(v)
    inverse = 3.0 / rho
    ux, uy, uz = mx * inverse, my * inverse, mz * inverse
    base = 1.0 - (ux * ux + uy * uy + uz * uz) * (1.0 / 6.0)
    along = {
        1: ux,
        3: uy,
        5: uz,
        7: ux + uy,
        9: ux - uy,
        11: ux + uz,
        13: ux - uz,
        15: uy + uz,
        17: uy - uz,
    }
    axis, diagonal = rho * (1.6 / 18.0), rho * (1.6 / 36.0)
    result = [rho * (1.6 / 3.0) * base - 0.6 * v[0]]
    for q in range(1, 19, 2):
        a = along[q]
        even = base + 0.5 * (a * a)
        factor = axis if q < 7 else diagonal
        result.append(factor * (even + a) - 0.6 * v[q])
        result.append(factor * (even - a) - 0.6 * v[q + 1])
    return result


def pull_back(v, b):
    rho, mx, my, mz = moments(v)
    inverse = 1.0 / rho
    ux, uy, uz = mx * inverse, my * inverse, mz * inverse
    s = {q: b[q] + b[q + 1] for q in range(1, 19, 2)}
    d = {q: b[q] - b[q + 1] for q in range(1, 19, 2)}
    for q in (1, 3, 5):
        s[q] = s[q] + s[q]
        d[q] = d[q] + d[q]
    sxy_p, sxz_p, syz_p = s[7] + s[9], s[11] + s[13], s[15] + s[17]
    sxy, sxz, syz = s[7] - s[9], s[11] - s[13], s[15] - s[17]
    s0 = 12.0 * b[0] + (s[1] + s[3]) + (s[5] + sxy_p) + (sxz_p + syz_p)
    sxx, syy, szz = s[1] + sxy_p + sxz_p, s[3] + sxy_p + syz_p, s[5] + sxz_p + syz_p
    s1x = d[1] + (d[7] + d[9]) + (d[11] + d[13])
    s1y = d[3] + (d[7] - d[9]) + (d[15] + d[17])
    s1z = d[5] + (d[11] - d[13]) + (d[15] - d[17])
    tx = sxx * ux + sxy * uy + sxz * uz
    ty = sxy * ux + syy * uy + syz * uz
    tz = sxz * ux + syz * uy + szz * uz
    k = 1.6 / 36.0
    square = ux * ux + uy * uy + uz * uz
    level = k * (s0 * (1.0 + 1.5 * square) - 4.5 * (ux * tx + uy * ty + uz * tz))
    gx = (3.0 * k) * (s1x + 3.0 * tx - ux * s0)
    gy = (3.0 * k) * (s1y + 3.0 * ty - uy * s0)
    gz = (3.0 * k) * (s1z + 3.0 * tz - uz * s0)
    along = {
        1: gx,
        3: gy,
        5: gz,
        7: gx + gy,
        9: gx - gy,
        11: gx + gz,
        13: gx - gz,
        15: gy + gz,
        17: gy - gz,
    }
    result = [level - 0.6 * b[0]]
    for q in range(1, 19, 2):
        result.append((level + along[q]) - 0.6 * b[q])
        result.append((level - along[q]) - 0.6 * b[q + 1])
    return result


SLOW, FAST = 0, 1
OUTER, MIDDLE, OTHER, ROWS = 0, 1, 2, 3
CELLS_IN, SEEDS_IN, SEED_FACES_IN = 12, 13, 14
CELLS_OUT, SLOW_OUT, REST_OUT = 0, 1, 2


def forward_kernel(
    start_ref, fluid_ref, seed_ref,
    state_ref, adjoint_ref,
    post_1, post_2, post_3, held, bits_ref, start, cells, solid,
    y_send, y_recv,
    load_sem, send_sem, recv_sem,
):
    _, nx, ny, nz = start_ref.shape
    tiles = ny // T
    last = tiles - 1
    top = PAD + ny
    me = {"gx": lax.axis_index("gx"), "gy": lax.axis_index("gy")}
    count = {"gx": lax.axis_size("gx"), "gy": lax.axis_size("gy")}
    odd = lax.rem(me["gx"], 2)
    sign = {SLOW: odd, FAST: 1 - odd}
    face = {side: (nx - 1) * p for side, p in sign.items()}
    rest = pl.ds(1 - odd, nx - 1)

    def first_of(p):
        return 6 - 5 * p

    def corner_of(p, up):
        return 8 - 6 * p if up else 7 - 4 * p

    def halo_of(p):
        return (nx + 1) * (1 - p)

    def device(dx, dy):
        to_x = lax.rem(me["gx"] + dx + count["gx"], count["gx"])
        to_y = lax.rem(me["gy"] + dy + count["gy"], count["gy"])
        return (to_x, to_y)

    def toward(side, dy):
        return device(2 * sign[side] - 1, dy)

    around = [(i, j) for i in (-1, 0, 1) for j in (-1, 0, 1) if (i, j) != (0, 0)]
    barrier = pltpu.get_barrier_semaphore()
    for i, j in around:
        pl.semaphore_signal(barrier, inc=1, device_id=device(i, j), device_id_type=pl.DeviceIdType.MESH)

    fluid_load = pltpu.make_async_copy(fluid_ref, cells, load_sem.at[0])
    fluid_load.start()
    slow_plane, fast_plane = pl.ds(face[SLOW], 1), pl.ds(face[FAST], 1)
    inner = pl.ds(1, nx - 2)
    start_load = [
        pltpu.make_async_copy(start_ref.at[:, planes, rows], start.at[:, planes, rows], load_sem.at[i])
        for i, planes, rows in (
            (1, slow_plane, pl.ds(0, ny)),
            (2, inner, pl.ds(0, T)),
            (2, inner, pl.ds(ny - T, T)),
            (2, fast_plane, pl.ds(0, ny)),
            (3, inner, pl.ds(T, ny - 2 * T)),
        )
    ]
    for load in start_load:
        load.start()
    seed_load = [
        pltpu.make_async_copy(
            seed_ref.at[q],
            held.at[SLOT[OPPOSITE[q]], pl.ds(1, nx), pl.ds(PAD, ny)],
            load_sem.at[4],
        )
        for q in range(19)
    ]

    def wait_rows(rows, sem):
        part, planes = next(
            (c, d)
            for c in range(ny + 2 * PAD, 0, -T)
            for d in range(nx + 2, 0, -1)
            if rows % (c * d) == 0 and rows <= 19 * c * d
        )
        view = post_1.at[pl.ds(0, rows // (part * planes)), pl.ds(0, planes), pl.ds(0, part)]
        pltpu.make_async_copy(view, view, sem).wait()

    def remote(source, target, out, into, to):
        return pltpu.make_async_remote_copy(
            src_ref=source, dst_ref=target, send_sem=send_sem.at[out], recv_sem=recv_sem.at[into],
            device_id=to, device_id_type=pl.DeviceIdType.MESH,
        )

    def lane(e, kind):
        return 4 * (e - 1) + kind

    seed_faces = {
        side: [
            remote(
                seed_ref.at[2 * k + 5 + p if k else 1 + p, face[side]],
                held.at[first_of(p) + k, halo_of(p), pl.ds(PAD, ny)],
                SLOW_OUT if side == SLOW else REST_OUT,
                SEED_FACES_IN if side == SLOW else SEEDS_IN,
                toward(side, 0),
            )
            for k in range(5)
        ]
        for side, p in sign.items()
    }

    def face_copy(into, ref, side, first_tile, end_tile):
        p = sign[side]
        five, rows = pl.ds(first_of(p), 5), pl.ds(PAD + T * first_tile, T * (end_tile - first_tile))
        return remote(
            ref.at[five, face[side] + 1, rows], ref.at[five, halo_of(p), rows],
            SLOW_OUT if side == SLOW else REST_OUT, into, toward(side, 0),
        )

    def row_copies(e, into, planes):
        return [
            remote(y_send.at[e, i, planes], y_recv.at[e, i, planes], REST_OUT, into, device(0, 1 - 2 * i))
            for i in range(2)
        ]

    ends = ((pl.ds(top - T, T), pl.ds(PAD - T, T)), (pl.ds(PAD, T), pl.ds(top, T)))

    def corner_copies(into, ref, side):
        p = sign[side]
        return [
            remote(
                ref.at[corner_of(p, i == 0), face[side] + 1, source],
                ref.at[corner_of(p, i == 0), halo_of(p), target],
                REST_OUT, into, toward(side, 1 - 2 * i),
            )
            for i, (source, target) in enumerate(ends)
        ]

    def pack_plane(e, ref, x):
        for k in range(5):
            y_send[e, 0, x, k] = ref[SLOT[UP[k]], x + 1, top - 1 : top, :]
            y_send[e, 1, x, k] = ref[SLOT[DOWN[k]], x + 1, PAD : PAD + 1, :]

    def unpack_plane(e, ref, x):
        for k in range(5):
            ref[SLOT[UP[k]], x + 1, PAD - 1 : PAD, :] = y_recv[e, 0, x, k]
            ref[SLOT[DOWN[k]], x + 1, top : top + 1, :] = y_recv[e, 1, x, k]

    def sweep(begin_at, length, body, unroll=True):
        def one(i, _):
            body(begin_at + i)
            return 0

        lax.fori_loop(0, length, one, 0, unroll=unroll)

    def begin(made):
        for copy in made:
            copy.start()

    turn = lax.rem(me["gx"] + 1, 4)

    def send_seeds(near):
        @pl.when(turn >= 2 if near else turn < 2)
        def _():
            begin(seed_faces[SLOW])

    fluid_load.wait()

    def to_float(x):
        solid[x + 1, PAD:top, :] = cells[x].astype(jnp.float32)
        y_send[0, 0, x, 0] = solid[x + 1, top - 1 : top, :]
        y_send[0, 1, x, 0] = solid[x + 1, PAD : PAD + 1, :]

    sweep(0, nx, to_float)
    pl.semaphore_wait(barrier, len(around))
    cell_copies = [
        remote(
            solid.at[face[side] + 1, source], solid.at[halo_of(sign[side]), target],
            CELLS_OUT, CELLS_IN, toward(side, dy),
        )
        for side in (SLOW, FAST)
        for dy, (source, target) in zip((0, 1, -1), ((pl.ds(PAD, ny),) * 2,) + ends)
    ]
    cell_copies += [
        remote(y_send.at[0, i, :, 0], y_recv.at[0, i, :, 0], CELLS_OUT, CELLS_IN, device(0, 1 - 2 * i))
        for i in range(2)
    ]
    cell_rows = 2 * (ny + 2 * T + nx)
    begin(cell_copies)

    def store(to, x, y, v, is_fluid):
        for q, value in enumerate(collide(v)):
            to[SLOT[q], x + 1, PAD + T * y : PAD + T * y + T, :] = jnp.where(
                is_fluid, value, v[OPPOSITE[q]]
            )

    def first(x, y):
        v = [start[q, x, T * y : T * y + T, :] for q in range(19)]
        store(post_1, x, y, v, solid[x + 1, PAD + T * y : PAD + T * y + T, :] > 0.5)

    def middle(source, to):
        def body(x, y):
            bits = bits_ref[x, T * y : T * y + T, :]
            v = stream(source, bits, x, y)
            store(to, x, y, v, (bits & 1) != 0)

        return body

    def edge_line(body):
        def line(x):
            body(x, 0)
            body(x, last)

        return line

    def inner_line(body):
        def line(x):
            for y in range(1, last):
                body(x, y)

        return line

    def sweep_edges(body):
        sweep(1 - odd, nx - 1, edge_line(body))

    def sweep_interior(body):
        sweep(1, nx - 2, inner_line(body), 1)

    def send_outer(e, to, body):
        outer = 4 - e
        into = lane(e, OUTER)
        for i in range(outer):
            body(face[SLOW], i)
            body(face[SLOW], last - i)
            if i == 0:
                begin(corner_copies(into, to, SLOW))
                pack_plane(e, to, face[SLOW])
                begin(row_copies(e, lane(e, ROWS), pl.ds(face[SLOW], 1)))
        begin([face_copy(into, to, SLOW, 0, outer), face_copy(into, to, SLOW, tiles - outer, tiles)])

    def take_outer(e):
        wait_rows(2 * T * (5 * (4 - e) + 1), recv_sem.at[lane(e, OUTER)])

    def send_middle(e, to, body):
        outer = 4 - e
        for y in range(outer, tiles - outer):
            body(face[SLOW], y)
        begin([face_copy(lane(e, MIDDLE), to, SLOW, outer, tiles - outer)])

    def take_middle(e):
        wait_rows(5 * T * (tiles - 2 * (4 - e)), recv_sem.at[lane(e, MIDDLE)])

    def send_edges(e, to, body):
        sweep_edges(body)
        begin(corner_copies(lane(e, OTHER), to, FAST))
        sweep(1 - odd, nx - 1, lambda x: pack_plane(e, to, x))
        begin(row_copies(e, lane(e, ROWS), rest))

    def send_fast(e, to, body):
        for y in range(1, last):
            body(face[FAST], y)
        begin([face_copy(lane(e, OTHER), to, FAST, 0, tiles)])

    def take_fast(e):
        wait_rows(5 * ny + 2 * T, recv_sem.at[lane(e, OTHER)])

    def take_rows(e, ref):
        wait_rows(10 * nx, recv_sem.at[lane(e, ROWS)])
        sweep(0, nx, lambda x: unpack_plane(e, ref, x))

    start_load[0].wait()
    send_outer(1, post_1, first)
    send_middle(1, post_1, first)
    send_seeds(False)
    wait_rows(19 * (2 * T * (nx - 2) + ny), load_sem.at[2])
    send_edges(1, post_1, first)
    send_fast(1, post_1, first)
    wait_rows(19 * (nx - 2) * (ny - 2 * T), load_sem.at[3])
    for load in seed_load:
        load.start()
    sweep_interior(first)

    layer = lax.broadcasted_iota(jnp.int32, (T, nz), 1)
    inside = {1: (layer > 0).astype(jnp.float32), -1: (layer < nz - 1).astype(jnp.float32)}

    def mark(x, y):
        flat, up, down = 1.0, 0.0, 0.0
        for q in range(1, 19):
            c = VELOCITY[q]
            row = PAD + T * y - c[1]
            tile = solid[x + 1 - c[0], row : row + T, :] * float(1 << q)
            if c[2] == 0:
                flat = flat + tile
            elif c[2] == 1:
                up = up + tile
            else:
                down = down + tile
        total = flat + pltpu.roll(up, 1, 1) * inside[1] + pltpu.roll(down, nz - 1, 1) * inside[-1]
        here = solid[x + 1, PAD + T * y : PAD + T * y + T, :]
        bits_ref[x, T * y : T * y + T, :] = (total * here).astype(jnp.int32)

    sweep_interior(mark)
    second = middle(post_1, post_2)
    sweep_interior(second)

    wait_rows(19 * nx * ny, load_sem.at[4])
    sweep(0, nx, lambda x: pack_plane(4, held, x))
    begin(row_copies(4, SEEDS_IN, pl.ds(0, nx)))
    begin(corner_copies(SEEDS_IN, held, SLOW) + corner_copies(SEEDS_IN, held, FAST))
    begin(seed_faces[FAST])

    wait_rows(cell_rows, recv_sem.at[CELLS_IN])

    def place_cells(x):
        solid[x + 1, PAD - 1 : PAD, :] = y_recv[0, 0, x, 0]
        solid[x + 1, top : top + 1, :] = y_recv[0, 1, x, 0]

    sweep(0, nx, place_cells)
    sweep(0, nx, edge_line(mark))
    sweep(0, 2, lambda i: inner_line(mark)(i * (nx - 1)))

    take_rows(1, post_1)
    take_fast(1)
    send_edges(2, post_2, second)
    send_fast(2, post_2, second)
    take_outer(1)
    send_outer(2, post_2, second)
    take_middle(1)
    send_middle(2, post_2, second)

    third = middle(post_2, post_3)
    sweep_interior(third)
    take_rows(2, post_2)
    take_fast(2)
    send_edges(3, post_3, third)
    send_fast(3, post_3, third)
    take_outer(2)
    send_outer(3, post_3, third)
    send_seeds(True)

    def final(x, y):
        rows = slice(T * y, T * y + T)
        bits = bits_ref[x, rows, :]
        v = stream(post_3, bits, x, y)
        for q in range(19):
            state_ref[q, x, rows, :] = v[q]
        turned = stream(held, bits, x, y)
        through = pull_back(v, [turned[OPPOSITE[q]] for q in range(19)])
        is_fluid = (bits & 1) != 0
        for q in range(19):
            adjoint_ref[q, x, rows, :] = jnp.where(is_fluid, through[q], turned[q])

    take_middle(2)
    send_middle(3, post_3, third)
    sweep_interior(final)
    wait_rows(5 * ny + 10 * nx + 4 * T, recv_sem.at[SEEDS_IN])
    sweep(0, nx, lambda x: unpack_plane(4, held, x))
    take_rows(3, post_3)
    take_fast(3)
    sweep_edges(final)
    for y in range(1, last):
        final(face[FAST], y)
    take_outer(3)
    take_middle(3)
    wait_rows(5 * ny, recv_sem.at[SEED_FACES_IN])
    for y in range(tiles):
        final(face[SLOW], y)
    wait_rows(cell_rows, send_sem.at[CELLS_OUT])
    wait_rows(4 * 5 * ny, send_sem.at[SLOW_OUT])
    wait_rows(4 * (5 * ny + 10 * nx + 4 * T), send_sem.at[REST_OUT])


def write_kernel(state_in, adjoint_in, state_ref, adjoint_ref, sem):
    pairs = ((state_in, state_ref), (adjoint_in, adjoint_ref))
    for i, (source, target) in enumerate(pairs):
        for q in range(source.shape[0]):
            pltpu.make_async_copy(source.at[q], target.at[q], sem.at[i]).start()
    for i, (source, target) in enumerate(pairs):
        pltpu.make_async_copy(source, target, sem.at[i]).wait()


def per_device(checkpoint, fluid, adjoint_in):
    n, nx, ny, nz = checkpoint.shape
    padded = (n, nx + 2, ny + 2 * PAD, nz)
    f32 = jnp.float32
    state, adjoint = pl.pallas_call(
        forward_kernel,
        out_shape=(
            pltpu.VMEM((n, nx, ny, nz), f32),
            pltpu.VMEM((n, nx, ny, nz), f32),
        ),
        in_specs=[pl.BlockSpec(memory_space=pltpu.HBM)] * 3,
        out_specs=[pl.BlockSpec(memory_space=pltpu.VMEM)] * 2,
        scratch_shapes=[
            pltpu.VMEM(padded, f32),
            pltpu.VMEM(padded, f32),
            pltpu.VMEM(padded, f32),
            pltpu.VMEM(padded, f32),
            pltpu.VMEM((nx, ny, nz), jnp.int32),
            pltpu.VMEM((n, nx, ny, nz), f32),
            pltpu.VMEM((nx, ny, nz), jnp.int32),
            pltpu.VMEM(padded[1:], f32),
            pltpu.VMEM((5, 2, nx, 5, 1, nz), f32),
            pltpu.VMEM((5, 2, nx, 5, 1, nz), f32),
            pltpu.SemaphoreType.DMA((5,)),
            pltpu.SemaphoreType.DMA((3,)),
            pltpu.SemaphoreType.DMA((15,)),
        ],
        compiler_params=pltpu.CompilerParams(
            collective_id=0, has_side_effects=True, vmem_limit_bytes=50 * MIB
        ),
        name="forward",
    )(checkpoint, fluid, adjoint_in)
    return pl.pallas_call(
        write_kernel,
        out_shape=(jax.ShapeDtypeStruct((n, nx, ny, nz), f32),) * 2,
        in_specs=[pl.BlockSpec(memory_space=pltpu.VMEM)] * 2,
        out_specs=[pl.BlockSpec(memory_space=pl.ANY)] * 2,
        scratch_shapes=[pltpu.SemaphoreType.DMA((2,))],
        compiler_params=pltpu.CompilerParams(vmem_limit_bytes=4 * MIB),
        name="write",
    )(state, adjoint)


def solution(mesh):
    return jax.shard_map(
        per_device,
        mesh=mesh,
        in_specs=(P(None, "gx", "gy", None), P("gx", "gy", None), P(None, "gx", "gy", None)),
        out_specs=(P(None, "gx", "gy", None), P(None, "gx", "gy", None)),
        check_vma=False,
    )
```

```python
import jax
import jax.numpy as jnp
from jax import lax
from jax.experimental import pallas as pl
from jax.experimental.pallas import tpu as pltpu
from jax.sharding import PartitionSpec as P

VELOCITY = [
    (0, 0, 0),
    (1, 0, 0),
    (-1, 0, 0),
    (0, 1, 0),
    (0, -1, 0),
    (0, 0, 1),
    (0, 0, -1),
    (1, 1, 0),
    (-1, -1, 0),
    (1, -1, 0),
    (-1, 1, 0),
    (1, 0, 1),
    (-1, 0, -1),
    (1, 0, -1),
    (-1, 0, 1),
    (0, 1, 1),
    (0, -1, -1),
    (0, 1, -1),
    (0, -1, 1),
]
OPPOSITE = [0, 2, 1, 4, 3, 6, 5, 8, 7, 10, 9, 12, 11, 14, 13, 16, 15, 18, 17]
ORDER = [0, 1, 7, 9, 11, 13, 2, 8, 10, 12, 14, 3, 4, 5, 6, 15, 16, 17, 18]
SLOT = [ORDER.index(q) for q in range(19)]
UP = [3, 7, 10, 15, 17]
DOWN = [4, 8, 9, 16, 18]
CORNER = [7, 8, 9, 10]
PAD = 8
T = 8
MIB = 1 << 20


def shifted(ref, q, x, y, speed):
    row = PAD + T * y - speed[1]
    tile = ref[SLOT[q], x + 1 - speed[0], row : row + T, :]
    if speed[2]:
        tile = pltpu.roll(tile, speed[2] % tile.shape[1], 1)
    return tile


def own(ref, q, x, y):
    return ref[SLOT[q], x + 1, PAD + T * y : PAD + T * y + T, :]


def stream(ref, bits, x, y):
    result = [own(ref, 0, x, y)]
    for q in range(1, 19):
        is_open = (bits & (1 << q)) != 0
        result.append(
            jnp.where(is_open, shifted(ref, q, x, y, VELOCITY[q]), own(ref, OPPOSITE[q], x, y))
        )
    return result


def moments(v):
    s = {q: v[q] + v[q + 1] for q in range(1, 19, 2)}
    d = {q: v[q] - v[q + 1] for q in range(1, 19, 2)}
    rho = v[0] + ((s[1] + s[3]) + (s[5] + s[7])) + ((s[9] + s[11]) + (s[13] + (s[15] + s[17])))
    mx = d[1] + (d[7] + d[9]) + (d[11] + d[13])
    my = d[3] + (d[7] - d[9]) + (d[15] + d[17])
    mz = d[5] + (d[11] - d[13]) + (d[15] - d[17])
    return rho, mx, my, mz


def collide(v):
    rho, mx, my, mz = moments(v)
    inverse = 3.0 / rho
    ux, uy, uz = mx * inverse, my * inverse, mz * inverse
    base = 1.0 - (ux * ux + uy * uy + uz * uz) * (1.0 / 6.0)
    along = {
        1: ux,
        3: uy,
        5: uz,
        7: ux + uy,
        9: ux - uy,
        11: ux + uz,
        13: ux - uz,
        15: uy + uz,
        17: uy - uz,
    }
    axis, diagonal = rho * (1.6 / 18.0), rho * (1.6 / 36.0)
    result = [rho * (1.6 / 3.0) * base - 0.6 * v[0]]
    for q in range(1, 19, 2):
        a = along[q]
        even = base + 0.5 * (a * a)
        factor = axis if q < 7 else diagonal
        result.append(factor * (even + a) - 0.6 * v[q])
        result.append(factor * (even - a) - 0.6 * v[q + 1])
    return result


def pull_back(v, b):
    rho, mx, my, mz = moments(v)
    inverse = 1.0 / rho
    ux, uy, uz = mx * inverse, my * inverse, mz * inverse
    s = {q: b[q] + b[q + 1] for q in range(1, 19, 2)}
    d = {q: b[q] - b[q + 1] for q in range(1, 19, 2)}
    for q in (1, 3, 5):
        s[q] = s[q] + s[q]
        d[q] = d[q] + d[q]
    sxy_p, sxz_p, syz_p = s[7] + s[9], s[11] + s[13], s[15] + s[17]
    sxy, sxz, syz = s[7] - s[9], s[11] - s[13], s[15] - s[17]
    s0 = 12.0 * b[0] + (s[1] + s[3]) + (s[5] + sxy_p) + (sxz_p + syz_p)
    sxx, syy, szz = s[1] + sxy_p + sxz_p, s[3] + sxy_p + syz_p, s[5] + sxz_p + syz_p
    s1x = d[1] + (d[7] + d[9]) + (d[11] + d[13])
    s1y = d[3] + (d[7] - d[9]) + (d[15] + d[17])
    s1z = d[5] + (d[11] - d[13]) + (d[15] - d[17])
    tx = sxx * ux + sxy * uy + sxz * uz
    ty = sxy * ux + syy * uy + syz * uz
    tz = sxz * ux + syz * uy + szz * uz
    k = 1.6 / 36.0
    square = ux * ux + uy * uy + uz * uz
    level = k * (s0 * (1.0 + 1.5 * square) - 4.5 * (ux * tx + uy * ty + uz * tz))
    gx = (3.0 * k) * (s1x + 3.0 * tx - ux * s0)
    gy = (3.0 * k) * (s1y + 3.0 * ty - uy * s0)
    gz = (3.0 * k) * (s1z + 3.0 * tz - uz * s0)
    along = {
        1: gx,
        3: gy,
        5: gz,
        7: gx + gy,
        9: gx - gy,
        11: gx + gz,
        13: gx - gz,
        15: gy + gz,
        17: gy - gz,
    }
    result = [level - 0.6 * b[0]]
    for q in range(1, 19, 2):
        result.append((level + along[q]) - 0.6 * b[q])
        result.append((level - along[q]) - 0.6 * b[q + 1])
    return result


def last_step(post, held, bits_ref, x, y):
    bits = bits_ref[x, T * y : T * y + T, :]
    v = stream(post, bits, x, y)
    turned = stream(held, bits, x, y)
    through = pull_back(v, [turned[OPPOSITE[q]] for q in range(19)])
    is_fluid = (bits & 1) != 0
    return v, [jnp.where(is_fluid, through[q], turned[q]) for q in range(19)]


SLOW, FAST = 0, 1
OUTER, MIDDLE, OTHER, ROWS = 0, 1, 2, 3
CELLS_IN, SEEDS_IN, SEED_FACES_IN = 12, 13, 14
CELLS_OUT, SLOW_OUT, REST_OUT = 0, 1, 2


def forward_kernel(
    start_ref, fluid_ref, seed_ref,
    state_ref, adjoint_ref, post_3, held, bits_ref,
    post_1, post_2, start, cells, solid,
    y_send, y_recv,
    load_sem, send_sem, recv_sem,
):
    _, nx, ny, nz = start_ref.shape
    tiles = ny // T
    last = tiles - 1
    top = PAD + ny
    me = {"gx": lax.axis_index("gx"), "gy": lax.axis_index("gy")}
    count = {"gx": lax.axis_size("gx"), "gy": lax.axis_size("gy")}
    odd = lax.rem(me["gx"], 2)
    sign = {SLOW: odd, FAST: 1 - odd}
    face = {side: (nx - 1) * p for side, p in sign.items()}
    rest = pl.ds(1 - odd, nx - 1)

    def first_of(p):
        return 6 - 5 * p

    def corner_of(p, up):
        return 8 - 6 * p if up else 7 - 4 * p

    def halo_of(p):
        return (nx + 1) * (1 - p)

    def device(dx, dy):
        to_x = lax.rem(me["gx"] + dx + count["gx"], count["gx"])
        to_y = lax.rem(me["gy"] + dy + count["gy"], count["gy"])
        return (to_x, to_y)

    def toward(side, dy):
        return device(2 * sign[side] - 1, dy)

    around = [(i, j) for i in (-1, 0, 1) for j in (-1, 0, 1) if (i, j) != (0, 0)]
    barrier = pltpu.get_barrier_semaphore()
    for i, j in around:
        pl.semaphore_signal(barrier, inc=1, device_id=device(i, j), device_id_type=pl.DeviceIdType.MESH)

    fluid_load = pltpu.make_async_copy(fluid_ref, cells, load_sem.at[0])
    fluid_load.start()
    slow_plane, fast_plane = pl.ds(face[SLOW], 1), pl.ds(face[FAST], 1)
    inner = pl.ds(1, nx - 2)
    start_load = [
        pltpu.make_async_copy(start_ref.at[:, planes, rows], start.at[:, planes, rows], load_sem.at[i])
        for i, planes, rows in (
            (1, slow_plane, pl.ds(0, ny)),
            (2, inner, pl.ds(0, T)),
            (2, inner, pl.ds(ny - T, T)),
            (2, fast_plane, pl.ds(0, ny)),
            (3, inner, pl.ds(T, ny - 2 * T)),
        )
    ]
    for load in start_load:
        load.start()
    seed_load = [
        pltpu.make_async_copy(
            seed_ref.at[q],
            held.at[SLOT[OPPOSITE[q]], pl.ds(1, nx), pl.ds(PAD, ny)],
            load_sem.at[4],
        )
        for q in range(19)
    ]

    def wait_rows(rows, sem):
        part, planes = next(
            (c, d)
            for c in range(ny + 2 * PAD, 0, -T)
            for d in range(nx + 2, 0, -1)
            if rows % (c * d) == 0 and rows <= 19 * c * d
        )
        view = post_1.at[pl.ds(0, rows // (part * planes)), pl.ds(0, planes), pl.ds(0, part)]
        pltpu.make_async_copy(view, view, sem).wait()

    def remote(source, target, out, into, to):
        return pltpu.make_async_remote_copy(
            src_ref=source, dst_ref=target, send_sem=send_sem.at[out], recv_sem=recv_sem.at[into],
            device_id=to, device_id_type=pl.DeviceIdType.MESH,
        )

    def lane(e, kind):
        return 4 * (e - 1) + kind

    seed_faces = {
        side: [
            remote(
                seed_ref.at[2 * k + 5 + p if k else 1 + p, face[side]],
                held.at[first_of(p) + k, halo_of(p), pl.ds(PAD, ny)],
                SLOW_OUT if side == SLOW else REST_OUT,
                SEED_FACES_IN if side == SLOW else SEEDS_IN,
                toward(side, 0),
            )
            for k in range(5)
        ]
        for side, p in sign.items()
    }

    def face_copy(into, ref, side, first_tile, end_tile):
        p = sign[side]
        five, rows = pl.ds(first_of(p), 5), pl.ds(PAD + T * first_tile, T * (end_tile - first_tile))
        return remote(
            ref.at[five, face[side] + 1, rows], ref.at[five, halo_of(p), rows],
            SLOW_OUT if side == SLOW else REST_OUT, into, toward(side, 0),
        )

    def row_copies(e, into, planes):
        return [
            remote(y_send.at[e, i, planes], y_recv.at[e, i, planes], REST_OUT, into, device(0, 1 - 2 * i))
            for i in range(2)
        ]

    ends = ((pl.ds(top - T, T), pl.ds(PAD - T, T)), (pl.ds(PAD, T), pl.ds(top, T)))

    def corner_copies(into, ref, side):
        p = sign[side]
        return [
            remote(
                ref.at[corner_of(p, i == 0), face[side] + 1, source],
                ref.at[corner_of(p, i == 0), halo_of(p), target],
                REST_OUT, into, toward(side, 1 - 2 * i),
            )
            for i, (source, target) in enumerate(ends)
        ]

    def pack_plane(e, ref, x):
        for k in range(5):
            y_send[e, 0, x, k] = ref[SLOT[UP[k]], x + 1, top - 1 : top, :]
            y_send[e, 1, x, k] = ref[SLOT[DOWN[k]], x + 1, PAD : PAD + 1, :]

    def unpack_plane(e, ref, x):
        for k in range(5):
            ref[SLOT[UP[k]], x + 1, PAD - 1 : PAD, :] = y_recv[e, 0, x, k]
            ref[SLOT[DOWN[k]], x + 1, top : top + 1, :] = y_recv[e, 1, x, k]

    def sweep(begin_at, length, body, unroll=True):
        def one(i, _):
            body(begin_at + i)
            return 0

        lax.fori_loop(0, length, one, 0, unroll=unroll)

    def begin(made):
        for copy in made:
            copy.start()

    turn = lax.rem(me["gx"] + 1, 4)

    def send_seeds(near):
        @pl.when(turn >= 2 if near else turn < 2)
        def _():
            begin(seed_faces[SLOW])

    fluid_load.wait()

    def to_float(x):
        solid[x + 1, PAD:top, :] = cells[x].astype(jnp.float32)
        y_send[0, 0, x, 0] = solid[x + 1, top - 1 : top, :]
        y_send[0, 1, x, 0] = solid[x + 1, PAD : PAD + 1, :]

    sweep(0, nx, to_float)
    pl.semaphore_wait(barrier, len(around))
    cell_copies = [
        remote(
            solid.at[face[side] + 1, source], solid.at[halo_of(sign[side]), target],
            CELLS_OUT, CELLS_IN, toward(side, dy),
        )
        for side in (SLOW, FAST)
        for dy, (source, target) in zip((0, 1, -1), ((pl.ds(PAD, ny),) * 2,) + ends)
    ]
    cell_copies += [
        remote(y_send.at[0, i, :, 0], y_recv.at[0, i, :, 0], CELLS_OUT, CELLS_IN, device(0, 1 - 2 * i))
        for i in range(2)
    ]
    cell_rows = 2 * (ny + 2 * T + nx)
    begin(cell_copies)

    def store(to, x, y, v, is_fluid):
        for q, value in enumerate(collide(v)):
            to[SLOT[q], x + 1, PAD + T * y : PAD + T * y + T, :] = jnp.where(
                is_fluid, value, v[OPPOSITE[q]]
            )

    def first(x, y):
        v = [start[q, x, T * y : T * y + T, :] for q in range(19)]
        store(post_1, x, y, v, solid[x + 1, PAD + T * y : PAD + T * y + T, :] > 0.5)

    def middle(source, to):
        def body(x, y):
            bits = bits_ref[x, T * y : T * y + T, :]
            v = stream(source, bits, x, y)
            store(to, x, y, v, (bits & 1) != 0)

        return body

    def edge_line(body):
        def line(x):
            body(x, 0)
            body(x, last)

        return line

    def inner_line(body):
        def line(x):
            for y in range(1, last):
                body(x, y)

        return line

    def sweep_edges(body):
        sweep(1 - odd, nx - 1, edge_line(body))

    def sweep_interior(body):
        sweep(1, nx - 2, inner_line(body), 1)

    def send_outer(e, to, body):
        outer = 4 - e
        into = lane(e, OUTER)
        for i in range(outer):
            body(face[SLOW], i)
            body(face[SLOW], last - i)
            if i == 0:
                begin(corner_copies(into, to, SLOW))
                pack_plane(e, to, face[SLOW])
                begin(row_copies(e, lane(e, ROWS), pl.ds(face[SLOW], 1)))
        begin([face_copy(into, to, SLOW, 0, outer), face_copy(into, to, SLOW, tiles - outer, tiles)])

    def take_outer(e):
        wait_rows(2 * T * (5 * (4 - e) + 1), recv_sem.at[lane(e, OUTER)])

    def send_middle(e, to, body):
        outer = 4 - e
        for y in range(outer, tiles - outer):
            body(face[SLOW], y)
        begin([face_copy(lane(e, MIDDLE), to, SLOW, outer, tiles - outer)])

    def take_middle(e):
        wait_rows(5 * T * (tiles - 2 * (4 - e)), recv_sem.at[lane(e, MIDDLE)])

    def send_edges(e, to, body):
        sweep_edges(body)
        begin(corner_copies(lane(e, OTHER), to, FAST))
        sweep(1 - odd, nx - 1, lambda x: pack_plane(e, to, x))
        begin(row_copies(e, lane(e, ROWS), rest))

    def send_fast(e, to, body):
        for y in range(1, last):
            body(face[FAST], y)
        begin([face_copy(lane(e, OTHER), to, FAST, 0, tiles)])

    def take_fast(e):
        wait_rows(5 * ny + 2 * T, recv_sem.at[lane(e, OTHER)])

    def take_rows(e, ref):
        wait_rows(10 * nx, recv_sem.at[lane(e, ROWS)])
        sweep(0, nx, lambda x: unpack_plane(e, ref, x))

    start_load[0].wait()
    send_outer(1, post_1, first)
    send_middle(1, post_1, first)
    send_seeds(False)
    wait_rows(19 * (2 * T * (nx - 2) + ny), load_sem.at[2])
    send_edges(1, post_1, first)
    send_fast(1, post_1, first)
    wait_rows(19 * (nx - 2) * (ny - 2 * T), load_sem.at[3])
    for load in seed_load:
        load.start()
    sweep_interior(first)

    layer = lax.broadcasted_iota(jnp.int32, (T, nz), 1)
    inside = {1: (layer > 0).astype(jnp.float32), -1: (layer < nz - 1).astype(jnp.float32)}

    def mark(x, y):
        flat, up, down = 1.0, 0.0, 0.0
        for q in range(1, 19):
            c = VELOCITY[q]
            row = PAD + T * y - c[1]
            tile = solid[x + 1 - c[0], row : row + T, :] * float(1 << q)
            if c[2] == 0:
                flat = flat + tile
            elif c[2] == 1:
                up = up + tile
            else:
                down = down + tile
        total = flat + pltpu.roll(up, 1, 1) * inside[1] + pltpu.roll(down, nz - 1, 1) * inside[-1]
        here = solid[x + 1, PAD + T * y : PAD + T * y + T, :]
        bits_ref[x, T * y : T * y + T, :] = (total * here).astype(jnp.int32)

    sweep_interior(mark)
    second = middle(post_1, post_2)
    sweep_interior(second)

    wait_rows(19 * nx * ny, load_sem.at[4])
    sweep(0, nx, lambda x: pack_plane(4, held, x))
    begin(row_copies(4, SEEDS_IN, pl.ds(0, nx)))
    begin(corner_copies(SEEDS_IN, held, SLOW) + corner_copies(SEEDS_IN, held, FAST))
    begin(seed_faces[FAST])

    wait_rows(cell_rows, recv_sem.at[CELLS_IN])

    def place_cells(x):
        solid[x + 1, PAD - 1 : PAD, :] = y_recv[0, 0, x, 0]
        solid[x + 1, top : top + 1, :] = y_recv[0, 1, x, 0]

    sweep(0, nx, place_cells)
    sweep(0, nx, edge_line(mark))
    sweep(0, 2, lambda i: inner_line(mark)(i * (nx - 1)))

    take_rows(1, post_1)
    take_fast(1)
    send_edges(2, post_2, second)
    send_fast(2, post_2, second)
    take_outer(1)
    send_outer(2, post_2, second)
    take_middle(1)
    send_middle(2, post_2, second)

    third = middle(post_2, post_3)
    sweep_interior(third)
    take_rows(2, post_2)
    take_fast(2)
    send_edges(3, post_3, third)
    send_fast(3, post_3, third)
    take_outer(2)
    send_outer(3, post_3, third)
    send_seeds(True)

    def final(x, y):
        rows = slice(T * y, T * y + T)
        v, through = last_step(post_3, held, bits_ref, x, y)
        for q in range(19):
            state_ref[q, x, rows, :] = v[q]
            adjoint_ref[q, x, rows, :] = through[q]

    take_middle(2)
    send_middle(3, post_3, third)
    sweep_interior(final)
    wait_rows(5 * ny + 10 * nx + 4 * T, recv_sem.at[SEEDS_IN])
    sweep(0, nx, lambda x: unpack_plane(4, held, x))
    take_rows(3, post_3)
    take_fast(3)
    sweep_edges(final)
    for y in range(1, last):
        final(face[FAST], y)
    take_outer(3)
    take_middle(3)
    wait_rows(5 * ny, recv_sem.at[SEED_FACES_IN])
    wait_rows(cell_rows, send_sem.at[CELLS_OUT])
    wait_rows(4 * 5 * ny, send_sem.at[SLOW_OUT])
    wait_rows(4 * (5 * ny + 10 * nx + 4 * T), send_sem.at[REST_OUT])


def write_kernel(
    state_in, adjoint_in, post, held, bits_ref, state_ref, adjoint_ref, state_face, adjoint_face, sem
):
    n, nx, ny, _ = state_in.shape
    odd = lax.rem(lax.axis_index("gx"), 2)
    slow = (nx - 1) * odd
    triples = ((state_in, state_face, state_ref), (adjoint_in, adjoint_face, adjoint_ref))
    rest = pl.ds(1 - odd, nx - 1)
    for i, (source, _, target) in enumerate(triples):
        for q in range(n):
            pltpu.make_async_copy(source.at[q, rest], target.at[q, rest], sem.at[i]).start()
    for y in range(ny // T):
        v, through = last_step(post, held, bits_ref, slow, y)
        for q in range(n):
            state_face[q, T * y : T * y + T, :] = v[q]
            adjoint_face[q, T * y : T * y + T, :] = through[q]
    faces = [
        pltpu.make_async_copy(source, target.at[:, slow], sem.at[2 + i])
        for i, (_, source, target) in enumerate(triples)
    ]
    for copy in faces:
        copy.start()
    for i, (source, _, target) in enumerate(triples):
        pltpu.make_async_copy(source.at[:, rest], target.at[:, rest], sem.at[i]).wait()
    for copy in faces:
        copy.wait()


def per_device(checkpoint, fluid, adjoint_in):
    n, nx, ny, nz = checkpoint.shape
    padded = (n, nx + 2, ny + 2 * PAD, nz)
    f32 = jnp.float32
    results = pl.pallas_call(
        forward_kernel,
        out_shape=(
            pltpu.VMEM((n, nx, ny, nz), f32),
            pltpu.VMEM((n, nx, ny, nz), f32),
            pltpu.VMEM(padded, f32),
            pltpu.VMEM(padded, f32),
            pltpu.VMEM((nx, ny, nz), jnp.int32),
        ),
        in_specs=[pl.BlockSpec(memory_space=pltpu.HBM)] * 3,
        out_specs=[pl.BlockSpec(memory_space=pltpu.VMEM)] * 5,
        scratch_shapes=[
            pltpu.VMEM(padded, f32),
            pltpu.VMEM(padded, f32),
            pltpu.VMEM((n, nx, ny, nz), f32),
            pltpu.VMEM((nx, ny, nz), jnp.int32),
            pltpu.VMEM(padded[1:], f32),
            pltpu.VMEM((5, 2, nx, 5, 1, nz), f32),
            pltpu.VMEM((5, 2, nx, 5, 1, nz), f32),
            pltpu.SemaphoreType.DMA((5,)),
            pltpu.SemaphoreType.DMA((3,)),
            pltpu.SemaphoreType.DMA((15,)),
        ],
        compiler_params=pltpu.CompilerParams(
            collective_id=0, has_side_effects=True, vmem_limit_bytes=30 * MIB
        ),
        name="forward",
    )(checkpoint, fluid, adjoint_in)
    return pl.pallas_call(
        write_kernel,
        out_shape=(jax.ShapeDtypeStruct((n, nx, ny, nz), f32),) * 2,
        in_specs=[pl.BlockSpec(memory_space=pltpu.VMEM)] * 5,
        out_specs=[pl.BlockSpec(memory_space=pl.ANY)] * 2,
        scratch_shapes=[
            pltpu.VMEM((n, ny, nz), f32),
            pltpu.VMEM((n, ny, nz), f32),
            pltpu.SemaphoreType.DMA((4,)),
        ],
        compiler_params=pltpu.CompilerParams(vmem_limit_bytes=4 * MIB),
        name="write",
    )(*results)


def solution(mesh):
    return jax.shard_map(
        per_device,
        mesh=mesh,
        in_specs=(P(None, "gx", "gy", None), P("gx", "gy", None), P(None, "gx", "gy", None)),
        out_specs=(P(None, "gx", "gy", None), P(None, "gx", "gy", None)),
        check_vma=False,
    )
```

```python
import jax
import jax.numpy as jnp
from jax import lax
from jax.experimental import pallas as pl
from jax.experimental.pallas import tpu as pltpu
from jax.sharding import PartitionSpec as P

VELOCITY = [
    (0, 0, 0),
    (1, 0, 0),
    (-1, 0, 0),
    (0, 1, 0),
    (0, -1, 0),
    (0, 0, 1),
    (0, 0, -1),
    (1, 1, 0),
    (-1, -1, 0),
    (1, -1, 0),
    (-1, 1, 0),
    (1, 0, 1),
    (-1, 0, -1),
    (1, 0, -1),
    (-1, 0, 1),
    (0, 1, 1),
    (0, -1, -1),
    (0, 1, -1),
    (0, -1, 1),
]
OPPOSITE = [0, 2, 1, 4, 3, 6, 5, 8, 7, 10, 9, 12, 11, 14, 13, 16, 15, 18, 17]
ORDER = [0, 1, 7, 9, 11, 13, 2, 8, 10, 12, 14, 3, 4, 5, 6, 15, 16, 17, 18]
SLOT = [ORDER.index(q) for q in range(19)]
UP = [3, 7, 10, 15, 17]
DOWN = [4, 8, 9, 16, 18]
CORNER = [7, 8, 9, 10]
PAD = 8
T = 8
MIB = 1 << 20


def shifted(ref, q, x, y, speed):
    row = PAD + T * y - speed[1]
    tile = ref[SLOT[q], x + 1 - speed[0], row : row + T, :]
    if speed[2]:
        tile = pltpu.roll(tile, speed[2] % tile.shape[1], 1)
    return tile


def own(ref, q, x, y):
    return ref[SLOT[q], x + 1, PAD + T * y : PAD + T * y + T, :]


def stream(ref, bits, x, y):
    result = [own(ref, 0, x, y)]
    for q in range(1, 19):
        is_open = (bits & (1 << q)) != 0
        result.append(
            jnp.where(is_open, shifted(ref, q, x, y, VELOCITY[q]), own(ref, OPPOSITE[q], x, y))
        )
    return result


def moments(v):
    s = {q: v[q] + v[q + 1] for q in range(1, 19, 2)}
    d = {q: v[q] - v[q + 1] for q in range(1, 19, 2)}
    rho = v[0] + ((s[1] + s[3]) + (s[5] + s[7])) + ((s[9] + s[11]) + (s[13] + (s[15] + s[17])))
    mx = d[1] + (d[7] + d[9]) + (d[11] + d[13])
    my = d[3] + (d[7] - d[9]) + (d[15] + d[17])
    mz = d[5] + (d[11] - d[13]) + (d[15] - d[17])
    return rho, mx, my, mz


def collide(v):
    rho, mx, my, mz = moments(v)
    inverse = 3.0 / rho
    ux, uy, uz = mx * inverse, my * inverse, mz * inverse
    base = 1.0 - (ux * ux + uy * uy + uz * uz) * (1.0 / 6.0)
    along = {
        1: ux,
        3: uy,
        5: uz,
        7: ux + uy,
        9: ux - uy,
        11: ux + uz,
        13: ux - uz,
        15: uy + uz,
        17: uy - uz,
    }
    axis, diagonal = rho * (1.6 / 18.0), rho * (1.6 / 36.0)
    result = [rho * (1.6 / 3.0) * base - 0.6 * v[0]]
    for q in range(1, 19, 2):
        a = along[q]
        even = base + 0.5 * (a * a)
        factor = axis if q < 7 else diagonal
        result.append(factor * (even + a) - 0.6 * v[q])
        result.append(factor * (even - a) - 0.6 * v[q + 1])
    return result


def pull_back(v, b):
    rho, mx, my, mz = moments(v)
    inverse = 1.0 / rho
    ux, uy, uz = mx * inverse, my * inverse, mz * inverse
    s = {q: b[q] + b[q + 1] for q in range(1, 19, 2)}
    d = {q: b[q] - b[q + 1] for q in range(1, 19, 2)}
    for q in (1, 3, 5):
        s[q] = s[q] + s[q]
        d[q] = d[q] + d[q]
    sxy_p, sxz_p, syz_p = s[7] + s[9], s[11] + s[13], s[15] + s[17]
    sxy, sxz, syz = s[7] - s[9], s[11] - s[13], s[15] - s[17]
    s0 = 12.0 * b[0] + (s[1] + s[3]) + (s[5] + sxy_p) + (sxz_p + syz_p)
    sxx, syy, szz = s[1] + sxy_p + sxz_p, s[3] + sxy_p + syz_p, s[5] + sxz_p + syz_p
    s1x = d[1] + (d[7] + d[9]) + (d[11] + d[13])
    s1y = d[3] + (d[7] - d[9]) + (d[15] + d[17])
    s1z = d[5] + (d[11] - d[13]) + (d[15] - d[17])
    tx = sxx * ux + sxy * uy + sxz * uz
    ty = sxy * ux + syy * uy + syz * uz
    tz = sxz * ux + syz * uy + szz * uz
    k = 1.6 / 36.0
    square = ux * ux + uy * uy + uz * uz
    level = k * (s0 * (1.0 + 1.5 * square) - 4.5 * (ux * tx + uy * ty + uz * tz))
    gx = (3.0 * k) * (s1x + 3.0 * tx - ux * s0)
    gy = (3.0 * k) * (s1y + 3.0 * ty - uy * s0)
    gz = (3.0 * k) * (s1z + 3.0 * tz - uz * s0)
    along = {
        1: gx,
        3: gy,
        5: gz,
        7: gx + gy,
        9: gx - gy,
        11: gx + gz,
        13: gx - gz,
        15: gy + gz,
        17: gy - gz,
    }
    result = [level - 0.6 * b[0]]
    for q in range(1, 19, 2):
        result.append((level + along[q]) - 0.6 * b[q])
        result.append((level - along[q]) - 0.6 * b[q + 1])
    return result


def last_step(post, held, bits_ref, x, y):
    bits = bits_ref[x, T * y : T * y + T, :]
    v = stream(post, bits, x, y)
    turned = stream(held, bits, x, y)
    through = pull_back(v, [turned[OPPOSITE[q]] for q in range(19)])
    is_fluid = (bits & 1) != 0
    return v, [jnp.where(is_fluid, through[q], turned[q]) for q in range(19)]


SLOW, FAST = 0, 1
OUTER, MIDDLE, OTHER, ROWS = 0, 1, 2, 3
CELLS_IN, SEEDS_IN, SEED_FACES_IN = 12, 13, 14
CELLS_OUT, SLOW_OUT, REST_OUT = 0, 1, 2


def forward_kernel(
    start_ref, fluid_ref, seed_ref,
    state_ref, adjoint_ref, post_3, held, bits_ref,
    post_1, post_2, start, cells, solid,
    y_send, y_recv,
    load_sem, send_sem, recv_sem,
):
    _, nx, ny, nz = start_ref.shape
    tiles = ny // T
    last = tiles - 1
    top = PAD + ny
    me = {"gx": lax.axis_index("gx"), "gy": lax.axis_index("gy")}
    count = {"gx": lax.axis_size("gx"), "gy": lax.axis_size("gy")}
    odd = lax.rem(me["gx"], 2)
    sign = {SLOW: odd, FAST: 1 - odd}
    face = {side: (nx - 1) * p for side, p in sign.items()}
    rest = pl.ds(1 - odd, nx - 1)

    def first_of(p):
        return 6 - 5 * p

    def corner_of(p, up):
        return 8 - 6 * p if up else 7 - 4 * p

    def halo_of(p):
        return (nx + 1) * (1 - p)

    def device(dx, dy):
        to_x = lax.rem(me["gx"] + dx + count["gx"], count["gx"])
        to_y = lax.rem(me["gy"] + dy + count["gy"], count["gy"])
        return (to_x, to_y)

    def toward(side, dy):
        return device(2 * sign[side] - 1, dy)

    around = [(i, j) for i in (-1, 0, 1) for j in (-1, 0, 1) if (i, j) != (0, 0)]
    barrier = pltpu.get_barrier_semaphore()
    for i, j in around:
        pl.semaphore_signal(barrier, inc=1, device_id=device(i, j), device_id_type=pl.DeviceIdType.MESH)

    fluid_load = pltpu.make_async_copy(fluid_ref, cells, load_sem.at[0])
    fluid_load.start()
    slow_plane, fast_plane = pl.ds(face[SLOW], 1), pl.ds(face[FAST], 1)
    inner = pl.ds(1, nx - 2)
    start_load = [
        pltpu.make_async_copy(start_ref.at[:, planes, rows], start.at[:, planes, rows], load_sem.at[i])
        for i, planes, rows in (
            (1, slow_plane, pl.ds(0, ny)),
            (2, inner, pl.ds(0, T)),
            (2, inner, pl.ds(ny - T, T)),
            (2, fast_plane, pl.ds(0, ny)),
            (3, inner, pl.ds(T, ny - 2 * T)),
        )
    ]
    for load in start_load:
        load.start()
    seed_load = [
        pltpu.make_async_copy(
            seed_ref.at[q],
            held.at[SLOT[OPPOSITE[q]], pl.ds(1, nx), pl.ds(PAD, ny)],
            load_sem.at[4],
        )
        for q in range(19)
    ]

    def wait_rows(rows, sem):
        part, planes = next(
            (c, d)
            for c in range(ny + 2 * PAD, 0, -T)
            for d in range(nx + 2, 0, -1)
            if rows % (c * d) == 0 and rows <= 19 * c * d
        )
        view = post_1.at[pl.ds(0, rows // (part * planes)), pl.ds(0, planes), pl.ds(0, part)]
        pltpu.make_async_copy(view, view, sem).wait()

    def remote(source, target, out, into, to):
        return pltpu.make_async_remote_copy(
            src_ref=source, dst_ref=target, send_sem=send_sem.at[out], recv_sem=recv_sem.at[into],
            device_id=to, device_id_type=pl.DeviceIdType.MESH,
        )

    def lane(e, kind):
        return 4 * (e - 1) + kind

    seed_faces = {
        side: [
            remote(
                seed_ref.at[2 * k + 5 + p if k else 1 + p, face[side]],
                held.at[first_of(p) + k, halo_of(p), pl.ds(PAD, ny)],
                SLOW_OUT if side == SLOW else REST_OUT,
                SEED_FACES_IN if side == SLOW else SEEDS_IN,
                toward(side, 0),
            )
            for k in range(5)
        ]
        for side, p in sign.items()
    }

    def face_copy(into, ref, side, first_tile, end_tile):
        p = sign[side]
        five, rows = pl.ds(first_of(p), 5), pl.ds(PAD + T * first_tile, T * (end_tile - first_tile))
        return remote(
            ref.at[five, face[side] + 1, rows], ref.at[five, halo_of(p), rows],
            SLOW_OUT if side == SLOW else REST_OUT, into, toward(side, 0),
        )

    def row_copies(e, into, planes):
        return [
            remote(y_send.at[e, i, planes], y_recv.at[e, i, planes], REST_OUT, into, device(0, 1 - 2 * i))
            for i in range(2)
        ]

    ends = ((pl.ds(top - T, T), pl.ds(PAD - T, T)), (pl.ds(PAD, T), pl.ds(top, T)))

    def corner_copies(into, ref, side):
        p = sign[side]
        return [
            remote(
                ref.at[corner_of(p, i == 0), face[side] + 1, source],
                ref.at[corner_of(p, i == 0), halo_of(p), target],
                REST_OUT, into, toward(side, 1 - 2 * i),
            )
            for i, (source, target) in enumerate(ends)
        ]

    def pack_plane(e, ref, x):
        for k in range(5):
            y_send[e, 0, x, k] = ref[SLOT[UP[k]], x + 1, top - 1 : top, :]
            y_send[e, 1, x, k] = ref[SLOT[DOWN[k]], x + 1, PAD : PAD + 1, :]

    def unpack_plane(e, ref, x):
        for k in range(5):
            ref[SLOT[UP[k]], x + 1, PAD - 1 : PAD, :] = y_recv[e, 0, x, k]
            ref[SLOT[DOWN[k]], x + 1, top : top + 1, :] = y_recv[e, 1, x, k]

    def sweep(begin_at, length, body, unroll=True):
        def one(i, _):
            body(begin_at + i)
            return 0

        lax.fori_loop(0, length, one, 0, unroll=unroll)

    def begin(made):
        for copy in made:
            copy.start()

    turn = lax.rem(me["gx"] + 1, 4)

    def send_seeds(near):
        @pl.when(turn >= 2 if near else turn < 2)
        def _():
            begin(seed_faces[SLOW])

    fluid_load.wait()

    def to_float(x):
        solid[x + 1, PAD:top, :] = cells[x].astype(jnp.float32)
        y_send[0, 0, x, 0] = solid[x + 1, top - 1 : top, :]
        y_send[0, 1, x, 0] = solid[x + 1, PAD : PAD + 1, :]

    sweep(0, nx, to_float)
    pl.semaphore_wait(barrier, len(around))
    cell_copies = [
        remote(
            solid.at[face[side] + 1, source], solid.at[halo_of(sign[side]), target],
            CELLS_OUT, CELLS_IN, toward(side, dy),
        )
        for side in (SLOW, FAST)
        for dy, (source, target) in zip((0, 1, -1), ((pl.ds(PAD, ny),) * 2,) + ends)
    ]
    cell_copies += [
        remote(y_send.at[0, i, :, 0], y_recv.at[0, i, :, 0], CELLS_OUT, CELLS_IN, device(0, 1 - 2 * i))
        for i in range(2)
    ]
    cell_rows = 2 * (ny + 2 * T + nx)
    begin(cell_copies)

    def store(to, x, y, v, is_fluid):
        for q, value in enumerate(collide(v)):
            to[SLOT[q], x + 1, PAD + T * y : PAD + T * y + T, :] = jnp.where(
                is_fluid, value, v[OPPOSITE[q]]
            )

    def first(x, y):
        v = [start[q, x, T * y : T * y + T, :] for q in range(19)]
        store(post_1, x, y, v, solid[x + 1, PAD + T * y : PAD + T * y + T, :] > 0.5)

    def middle(source, to):
        def body(x, y):
            bits = bits_ref[x, T * y : T * y + T, :]
            v = stream(source, bits, x, y)
            store(to, x, y, v, (bits & 1) != 0)

        return body

    def edge_line(body):
        def line(x):
            body(x, 0)
            body(x, last)

        return line

    def inner_line(body):
        def line(x):
            for y in range(1, last):
                body(x, y)

        return line

    def sweep_edges(body):
        sweep(1 - odd, nx - 1, edge_line(body))

    def sweep_interior(body):
        sweep(1, nx - 2, inner_line(body), 1)

    def send_outer(e, to, body):
        outer = 4 - e
        into = lane(e, OUTER)
        for i in range(outer):
            body(face[SLOW], i)
            body(face[SLOW], last - i)
            if i == 0:
                begin(corner_copies(into, to, SLOW))
                pack_plane(e, to, face[SLOW])
                begin(row_copies(e, lane(e, ROWS), pl.ds(face[SLOW], 1)))
        begin([face_copy(into, to, SLOW, 0, outer), face_copy(into, to, SLOW, tiles - outer, tiles)])

    def take_outer(e):
        wait_rows(2 * T * (5 * (4 - e) + 1), recv_sem.at[lane(e, OUTER)])

    def send_middle(e, to, body):
        outer = 4 - e
        for y in range(outer, tiles - outer):
            body(face[SLOW], y)
        begin([face_copy(lane(e, MIDDLE), to, SLOW, outer, tiles - outer)])

    def take_middle(e):
        wait_rows(5 * T * (tiles - 2 * (4 - e)), recv_sem.at[lane(e, MIDDLE)])

    def send_edges(e, to, body):
        sweep_edges(body)
        begin(corner_copies(lane(e, OTHER), to, FAST))
        sweep(1 - odd, nx - 1, lambda x: pack_plane(e, to, x))
        begin(row_copies(e, lane(e, ROWS), rest))

    def send_fast(e, to, body):
        for y in range(1, last):
            body(face[FAST], y)
        begin([face_copy(lane(e, OTHER), to, FAST, 0, tiles)])

    def take_fast(e):
        wait_rows(5 * ny + 2 * T, recv_sem.at[lane(e, OTHER)])

    def take_rows(e, ref):
        wait_rows(10 * nx, recv_sem.at[lane(e, ROWS)])
        sweep(0, nx, lambda x: unpack_plane(e, ref, x))

    start_load[0].wait()
    send_outer(1, post_1, first)
    send_middle(1, post_1, first)
    send_seeds(False)
    wait_rows(19 * (2 * T * (nx - 2) + ny), load_sem.at[2])
    send_edges(1, post_1, first)
    send_fast(1, post_1, first)
    wait_rows(19 * (nx - 2) * (ny - 2 * T), load_sem.at[3])
    for load in seed_load:
        load.start()
    sweep_interior(first)

    layer = lax.broadcasted_iota(jnp.int32, (T, nz), 1)
    inside = {1: (layer > 0).astype(jnp.float32), -1: (layer < nz - 1).astype(jnp.float32)}

    def mark(x, y):
        flat, up, down = 1.0, 0.0, 0.0
        for q in range(1, 19):
            c = VELOCITY[q]
            row = PAD + T * y - c[1]
            tile = solid[x + 1 - c[0], row : row + T, :] * float(1 << q)
            if c[2] == 0:
                flat = flat + tile
            elif c[2] == 1:
                up = up + tile
            else:
                down = down + tile
        total = flat + pltpu.roll(up, 1, 1) * inside[1] + pltpu.roll(down, nz - 1, 1) * inside[-1]
        here = solid[x + 1, PAD + T * y : PAD + T * y + T, :]
        bits_ref[x, T * y : T * y + T, :] = (total * here).astype(jnp.int32)

    sweep_interior(mark)
    second = middle(post_1, post_2)
    sweep_interior(second)

    wait_rows(19 * nx * ny, load_sem.at[4])
    sweep(0, nx, lambda x: pack_plane(4, held, x))
    begin(row_copies(4, SEEDS_IN, pl.ds(0, nx)))
    begin(corner_copies(SEEDS_IN, held, SLOW) + corner_copies(SEEDS_IN, held, FAST))
    begin(seed_faces[FAST])

    wait_rows(cell_rows, recv_sem.at[CELLS_IN])

    def place_cells(x):
        solid[x + 1, PAD - 1 : PAD, :] = y_recv[0, 0, x, 0]
        solid[x + 1, top : top + 1, :] = y_recv[0, 1, x, 0]

    sweep(0, nx, place_cells)
    sweep(0, nx, edge_line(mark))
    sweep(0, 2, lambda i: inner_line(mark)(i * (nx - 1)))

    take_rows(1, post_1)
    take_fast(1)
    send_edges(2, post_2, second)
    take_outer(1)
    send_outer(2, post_2, second)
    send_fast(2, post_2, second)
    take_middle(1)
    send_middle(2, post_2, second)

    third = middle(post_2, post_3)
    sweep_interior(third)
    take_rows(2, post_2)
    take_fast(2)
    send_edges(3, post_3, third)
    take_outer(2)
    send_outer(3, post_3, third)
    send_fast(3, post_3, third)
    send_seeds(True)

    def final(x, y):
        rows = slice(T * y, T * y + T)
        v, through = last_step(post_3, held, bits_ref, x, y)
        for q in range(19):
            state_ref[q, x, rows, :] = v[q]
            adjoint_ref[q, x, rows, :] = through[q]

    take_middle(2)
    send_middle(3, post_3, third)
    sweep_interior(final)
    wait_rows(5 * ny + 10 * nx + 4 * T, recv_sem.at[SEEDS_IN])
    sweep(0, nx, lambda x: unpack_plane(4, held, x))
    take_rows(3, post_3)
    take_fast(3)
    sweep_edges(final)
    for y in range(1, last):
        final(face[FAST], y)
    take_outer(3)
    take_middle(3)
    wait_rows(5 * ny, recv_sem.at[SEED_FACES_IN])
    wait_rows(cell_rows, send_sem.at[CELLS_OUT])
    wait_rows(4 * 5 * ny, send_sem.at[SLOW_OUT])
    wait_rows(4 * (5 * ny + 10 * nx + 4 * T), send_sem.at[REST_OUT])


def write_kernel(
    state_in, adjoint_in, post, held, bits_ref, state_ref, adjoint_ref, state_face, adjoint_face, sem
):
    n, nx, ny, _ = state_in.shape
    odd = lax.rem(lax.axis_index("gx"), 2)
    slow = (nx - 1) * odd
    triples = ((state_in, state_face, state_ref), (adjoint_in, adjoint_face, adjoint_ref))
    rest = pl.ds(1 - odd, nx - 1)
    for i, (source, _, target) in enumerate(triples):
        for q in range(n):
            pltpu.make_async_copy(source.at[q, rest], target.at[q, rest], sem.at[i]).start()
    for y in range(ny // T):
        v, through = last_step(post, held, bits_ref, slow, y)
        for q in range(n):
            state_face[q, T * y : T * y + T, :] = v[q]
            adjoint_face[q, T * y : T * y + T, :] = through[q]
    faces = [
        pltpu.make_async_copy(source, target.at[:, slow], sem.at[2 + i])
        for i, (_, source, target) in enumerate(triples)
    ]
    for copy in faces:
        copy.start()
    for i, (source, _, target) in enumerate(triples):
        pltpu.make_async_copy(source.at[:, rest], target.at[:, rest], sem.at[i]).wait()
    for copy in faces:
        copy.wait()


def per_device(checkpoint, fluid, adjoint_in):
    n, nx, ny, nz = checkpoint.shape
    padded = (n, nx + 2, ny + 2 * PAD, nz)
    f32 = jnp.float32
    results = pl.pallas_call(
        forward_kernel,
        out_shape=(
            pltpu.VMEM((n, nx, ny, nz), f32),
            pltpu.VMEM((n, nx, ny, nz), f32),
            pltpu.VMEM(padded, f32),
            pltpu.VMEM(padded, f32),
            pltpu.VMEM((nx, ny, nz), jnp.int32),
        ),
        in_specs=[pl.BlockSpec(memory_space=pltpu.HBM)] * 3,
        out_specs=[pl.BlockSpec(memory_space=pltpu.VMEM)] * 5,
        scratch_shapes=[
            pltpu.VMEM(padded, f32),
            pltpu.VMEM(padded, f32),
            pltpu.VMEM((n, nx, ny, nz), f32),
            pltpu.VMEM((nx, ny, nz), jnp.int32),
            pltpu.VMEM(padded[1:], f32),
            pltpu.VMEM((5, 2, nx, 5, 1, nz), f32),
            pltpu.VMEM((5, 2, nx, 5, 1, nz), f32),
            pltpu.SemaphoreType.DMA((5,)),
            pltpu.SemaphoreType.DMA((3,)),
            pltpu.SemaphoreType.DMA((15,)),
        ],
        compiler_params=pltpu.CompilerParams(
            collective_id=0, has_side_effects=True, vmem_limit_bytes=30 * MIB
        ),
        name="forward",
    )(checkpoint, fluid, adjoint_in)
    return pl.pallas_call(
        write_kernel,
        out_shape=(jax.ShapeDtypeStruct((n, nx, ny, nz), f32),) * 2,
        in_specs=[pl.BlockSpec(memory_space=pltpu.VMEM)] * 5,
        out_specs=[pl.BlockSpec(memory_space=pl.ANY)] * 2,
        scratch_shapes=[
            pltpu.VMEM((n, ny, nz), f32),
            pltpu.VMEM((n, ny, nz), f32),
            pltpu.SemaphoreType.DMA((4,)),
        ],
        compiler_params=pltpu.CompilerParams(vmem_limit_bytes=4 * MIB),
        name="write",
    )(*results)


def solution(mesh):
    return jax.shard_map(
        per_device,
        mesh=mesh,
        in_specs=(P(None, "gx", "gy", None), P("gx", "gy", None), P(None, "gx", "gy", None)),
        out_specs=(P(None, "gx", "gy", None), P(None, "gx", "gy", None)),
        check_vma=False,
    )
```
